512 devices in a mesh: dp: 8 (over x, core), expert: 64 (over y, z).
Axes of the slice: x: 4, y: 4, z: 16, core: 2. Of those that a mesh axis runs over, the one named last changes fastest.
Arguments:
- tokens_in: bfloat16 [65536, 3584], P(('dp', 'expert')), may hold values from -6 to 6
- out_grad: bfloat16 [65536, 3584], P(('dp', 'expert')), may hold values from -0.59765625 to 0.59765625
- router_logits: float32 [65536, 192], P(('dp', 'expert')), may hold values from -12 to 250
- expert_ids: int32 [65536, 8], P(('dp', 'expert')), may hold values from 0 to 191, all different within a row; in each aligned block of 128 rows (0 to 127, 128 to 255, ...) at most 8 rows name the same one
- saved_hidden: bfloat16 [8, 64, 64, 8, 1024], P('dp', 'expert'), may hold values from -6 to 6
- down_weight: bfloat16 [64, 1024, 3584], P('expert', 'dp'), may hold values from -0.1875 to 0.1875
Outputs:
- hidden_grad: bfloat16 [8, 64, 64, 8, 1024], P('dp', 'expert')
- logit_grad: float32 [65536, 192], P(('dp', 'expert'))
- router_grad: float32 [3584, 192], P('expert', 'dp')
The draws below stay inside these ranges and needn't reach their ends.
Inputs may be any that keep to these rules, and one draw needn't show every extreme that they name: `expert_ids`: among the 128 rows of one device no expert is named by more than 8 rows, a bound that some block reaches.
All inputs are finite; a program needn't handle non-finite values.
Results may differ from the reference program's by a relative error of at most 0.013.
Values may be sent and summed in bfloat16 or wider, within the bound.
A program may use at most 64 MiB of HBM per device.

```python
import math
import jax
import jax.numpy as jnp
import numpy as np
from jax import lax

D = 3584
FW = 1024
EXPERTS = 192
TOPK = 8
TOK_DEV = 128
CAP = 8
TOKENS = 65536
N_DP = 8
N_EXPERT = 64


def draw_router_logits(key, part):
    first_key = jax.random.fold_in(key, 0)
    base = jnp.clip(2.0 * jax.random.normal(first_key, (TOKENS, EXPERTS), jnp.float32), -12.0, 12.0)
    return base


def steps_of(own_key, dims, pieces, least, top_value):
    level = 1.0
    for position, blocks in pieces:
        draws = jax.random.uniform(jax.random.fold_in(jax.random.fold_in(own_key, 6), position), (blocks,), jnp.float32, least / len(pieces), top_value / len(pieces))
        level = level * jnp.repeat(jnp.exp(draws), dims[position] // blocks).reshape((-1,) + (1,) * (len(dims) - 1 - position))
    return level


def routed_block(own_key, own, number, rows, count, top, reach, slope):
    order = jax.random.permutation(own_key, count)
    heavy_load, common = portions_of(count, rows * top, reach, slope, True), portions_of(count, rows * top, reach, slope, False)
    places = jnp.arange(count)

    def named(lengths, rotation):
        used = int((lengths > 0).sum())
        fixed = max(1, used // 4)
        moved = fixed + (places - fixed + rotation * (used - fixed)) % max(1, count - fixed)
        return jnp.zeros((count,), jnp.int32).at[order[jnp.where(places < fixed, places, moved)]].set(jnp.asarray(lengths, jnp.int32))

    lengths = jnp.where(number % 4 == 0, named(heavy_load, number // 4), named(common, number - number // 4 - 1))
    mixed = jax.random.permutation(jax.random.fold_in(own, 3), count)
    giver, sink = mixed[0:count // 2 * 2:2], mixed[1:count // 2 * 2:2]
    slack = jnp.minimum(lengths[giver] - 1, reach - lengths[sink]) // 2
    slack = jnp.where((giver == order[0]) | (sink == order[0]) | (lengths[sink] == 0), 0, jnp.maximum(slack, 0))
    moved = jax.random.randint(jax.random.fold_in(own, 4), (count // 2,), 0, 1 << 20) % (slack + 1)
    lengths = lengths.at[giver].add(-moved).at[sink].add(moved)
    labels = jnp.searchsorted(jnp.cumsum(lengths), jnp.arange(rows * top), side="right").astype(jnp.int32)
    grid = labels.reshape(top, rows).T
    grid = grid[jax.random.permutation(jax.random.fold_in(own, 1), rows)]
    rotation = jax.random.randint(jax.random.fold_in(own, 2), (rows, 1), 0, top)
    return jnp.take_along_axis(grid, (jnp.arange(top)[None, :] + rotation) % top, axis=1)


def portions_of(amount, total, reach, skew, full):
    weights = [(1 << 20) // math.isqrt(grade ** skew) + 1 for grade in range(1, amount + 1)]
    largest = reach if full else min(reach, max(-(-total // amount), total * weights[0] // sum(weights)))
    least = 1 if total - largest >= amount - 1 else 0
    given, surplus = [largest] + [least] * (amount - 1), total - largest - least * (amount - 1)
    while surplus > 0:
        free = [i for i in range(1, amount) if given[i] < largest] or [i for i in range(1, amount) if given[i] < reach]
        pool, budget = sum([weights[i] for i in free]), surplus
        for i in free:
            addition = min(reach - given[i], max(1, budget * weights[i] // pool), surplus)
            given[i] = given[i] + addition
            surplus = surplus - addition
    return np.array(given)


def centred(key, shape, deviation, reach, cuts=(), held_as=jnp.bfloat16):
    result = jax.random.normal(key, shape, jnp.float32) * deviation
    if len(cuts) > 0:
        result = steps_of(key, shape, cuts, -0.22, 0.18) * result
    return jnp.clip(result, min=-reach, max=reach).astype(held_as)


def setup_inputs(seed: int = 0) -> dict:
    key_list = jax.random.split(jax.random.key(seed), 7)
    tokens_in = centred(key_list[0], (TOKENS, D), 1.0, 6.0, ((0, 512),))
    out_grad = centred(key_list[1], (TOKENS, D), 0.1, 0.59765625, ((0, 512),))
    router_logits = draw_router_logits(jax.random.fold_in(key_list[6], 71), 0)
    expert_ids_keys = jax.random.split(jax.random.fold_in(key_list[3], 1), TOKENS // TOK_DEV)
    expert_ids_turns = jax.random.permutation(jax.random.fold_in(key_list[3], 3), TOKENS // TOK_DEV)
    expert_ids = jax.vmap(lambda own, number: routed_block(jax.random.fold_in(key_list[3], 2), own, number, TOK_DEV, EXPERTS, TOPK, CAP, 2))(expert_ids_keys, expert_ids_turns).reshape((TOKENS, TOPK))
    saved_hidden = centred(key_list[4], (N_DP, N_EXPERT, N_EXPERT, CAP, FW), 1.0, 6.0, ((0, 8), (1, 64)))
    down_weight = centred(key_list[5], (N_EXPERT, FW, D), FW ** -0.5, 0.1875, ((0, 64), (1, 8)))
    return dict(tokens_in=tokens_in, out_grad=out_grad, router_logits=router_logits, expert_ids=expert_ids, saved_hidden=saved_hidden, down_weight=down_weight)


RSCALE = 2.827
ZLOSS = 0.25


def slot_table(ids_block, flight, cap):
    owners = jnp.arange(flight, dtype=jnp.int32)
    chosen = jnp.any(ids_block[:, :, None] == owners[None, None, :], axis=1)
    as_int = chosen.astype(jnp.int32)
    rank = jnp.cumsum(as_int, axis=0) - as_int
    places = jnp.arange(cap, dtype=jnp.int32)
    table = chosen[None, :, :] & (rank[None, :, :] == places[:, None, None])
    return jnp.transpose(table, (2, 0, 1))


def gate_parts(logits, ids):
    top = jnp.max(logits, axis=1, keepdims=True)
    shifted = jnp.exp(logits - top)
    total = jnp.sum(shifted, axis=1, keepdims=True)
    probs = shifted / total
    lse = top + jnp.log(total)
    columns = jnp.arange(logits.shape[1], dtype=jnp.int32)
    picks = (ids[:, :, None] == columns[None, None, :]).astype(jnp.float32)
    chosen_logit = jnp.sum(picks * logits[:, None, :], axis=2)
    scores = jax.nn.sigmoid(chosen_logit)
    ssum = jnp.sum(scores, axis=1, keepdims=True)
    gates = RSCALE * scores / ssum
    return probs, lse, picks, scores, ssum, gates


def reference(tokens_in, out_grad, router_logits, expert_ids, saved_hidden, down_weight):
    rows = TOK_DEV * N_EXPERT
    highest = lax.Precision.HIGHEST

    def group(index):
        start = index * rows
        xin = lax.dynamic_slice_in_dim(tokens_in, start, rows, 0)
        dyin = lax.dynamic_slice_in_dim(out_grad, start, rows, 0)
        logits = lax.dynamic_slice_in_dim(router_logits, start, rows, 0)
        ids = lax.dynamic_slice_in_dim(expert_ids, start, rows, 0)
        probs, lse, picks, scores, ssum, gates = gate_parts(logits, ids)
        gate_half = gates.astype(jnp.bfloat16)
        in_window = picks[:, :, :N_EXPERT]
        gate_te = jnp.sum(in_window * gate_half.astype(jnp.float32)[:, :, None], axis=1)
        gate_blocks = gate_te.reshape(N_EXPERT, TOK_DEV, N_EXPERT)
        tables = jax.vmap(lambda blk: slot_table(blk, N_EXPERT, CAP))(ids.reshape(N_EXPERT, TOK_DEV, TOPK))
        dy_blocks = dyin.astype(jnp.float32).reshape(N_EXPERT, TOK_DEV, D)
        hidden_here = saved_hidden[index]

        def owner(expert):
            tab = tables[:, expert].astype(jnp.float32)
            recv = jnp.einsum('sct,std->scd', tab, dy_blocks, precision=highest).astype(jnp.bfloat16)
            weight = down_weight[expert]
            grads = jnp.dot(recv.reshape(N_EXPERT * CAP, D), weight.T, preferred_element_type=jnp.float32)
            gslot = jnp.einsum('sct,st->sc', tab, gate_blocks[:, :, expert], precision=highest)
            dhid = (gslot.reshape(-1, 1) * grads).astype(jnp.bfloat16).reshape(N_EXPERT, CAP, FW)
            saved = hidden_here[expert].reshape(N_EXPERT * CAP, FW).astype(jnp.float32)
            dgate = jnp.sum(saved * grads, axis=1).reshape(N_EXPERT, CAP)
            back = jnp.einsum('sct,sc->st', tab, dgate, precision=highest)
            return dhid, back

        dhid_all, back_all = lax.map(owner, jnp.arange(N_EXPERT, dtype=jnp.int32))
        grad_te = jnp.transpose(back_all, (1, 2, 0)).reshape(rows, N_EXPERT)
        grad_choice = jnp.sum(in_window * grad_te[:, None, :], axis=2)
        mixed = jnp.sum(grad_choice * gates, axis=1, keepdims=True) / RSCALE
        dscore = (RSCALE / ssum) * (grad_choice - mixed)
        dchosen = dscore * scores * (1.0 - scores)
        lgrad = jnp.sum(picks * dchosen[:, :, None], axis=1) + 2.0 * ZLOSS * lse * probs
        panel = jnp.dot(xin.astype(jnp.float32).T, lgrad, precision=highest)
        return dhid_all, lgrad, panel

    dhid, lgrad, panels = lax.map(group, jnp.arange(N_DP, dtype=jnp.int32))
    return dhid, lgrad.reshape(TOKENS, EXPERTS), jnp.sum(panels, axis=0)
```

```python
import functools

import jax
import jax.numpy as jnp
from jax import lax
from jax.experimental import pallas as pl
from jax.experimental.pallas import tpu as pltpu
from jax.sharding import PartitionSpec as P

RSCALE = 2.827
ZLOSS = 0.25
NC = 2
MESH = pl.DeviceIdType.MESH
F32 = jnp.float32
BF16 = jnp.bfloat16


def drain(ref, sem):
    pltpu.make_async_copy(ref, ref, sem).wait()


def iota(shape, dim):
    return lax.broadcasted_iota(jnp.int32, shape, dim)


def kernel(
    dims,
    og, logits, ids, tok, w, saved,
    hid, lg, rg,
    send, recv, wfull, tokg, savedv, gsend, grecv, rsend, rrecv, lgs, lgb, lhs, zsend, zrecv, zterm, posv, small,
    row_r, row_s, gate_r, gate_s, ret_r, ret_s, wx_s, wx_r, wc_s, wc_r,
    t1_s, t1_r, tx_s, tx_r, tc_s, tc_r, lg_s, lg_r, z_s, z_r, local_sem,
):
    NX, NY, NZ = dims
    NDP, NE, NG = NX * NC, NY * NZ, NZ // 2
    GS = NY * 2
    D = og.shape[1]
    H = D // 2
    Q = D // NY
    FW = wfull.shape[0]
    FS = FW // NDP
    EX = logits.shape[1]
    ED = EX // NDP
    R = D // NE
    dp, e = lax.axis_index("dp"), lax.axis_index("expert")
    x, core = dp // NC, dp % NC
    y, z = e // NZ, e % NZ
    m0 = z // 2
    place = m0 * GS + y * 2 + z % 2

    def remote(src, dst, s, r, dev):
        return pltpu.make_async_remote_copy(
            src_ref=src, dst_ref=dst, send_sem=s, recv_sem=r, device_id=dev, device_id_type=MESH
        )

    barrier = pltpu.get_barrier_semaphore()

    def greet(i, c):
        pl.semaphore_signal(barrier, inc=1, device_id=(dp, lax.rem(e + i, NE)), device_id_type=MESH)
        return c

    lax.fori_loop(1, NE, greet, 0)

    def greet2(i, c):
        other = lax.rem(dp + 1 + i // NY, NDP)
        pl.semaphore_signal(barrier, inc=1, device_id=(other, lax.rem(i, NY) * NZ + z), device_id_type=MESH)
        return c

    lax.fori_loop(0, (NDP - 1) * NY, greet2, 0)
    load = pltpu.make_async_copy(saved, savedv, local_sem.at[0])
    load.start()
    own_w = pltpu.make_async_copy(w, wfull.at[pl.ds(pl.multiple_of(dp * FS, FS), FS)], local_sem.at[1])
    own_w.start()

    full = logits[...]
    if EX > 128:
        lt = jnp.concatenate([full[:, :128].T, full[:, EX - 128 :].T[256 - EX :]], axis=0)
    else:
        lt = full.T
    top = jnp.max(lt, axis=0, keepdims=True)
    shifted = jnp.exp(lt - top)
    total = jnp.sum(shifted, axis=0, keepdims=True)
    lse = top + jnp.log(total)
    zterm[...] = (2.0 * ZLOSS) * lse * (shifted / total)
    T = lt.shape[1]
    names = iota((EX, T), 0)
    k_rows = [ids[k : k + 1, :] for k in range(ids.shape[0])]
    chosen = jnp.concatenate(
        [jnp.sum(jnp.where(names == row, lt, 0.0), axis=0, keepdims=True) for row in k_rows], axis=0
    )
    scores = 1.0 / (1.0 + jnp.exp(-chosen))
    ssum = jnp.sum(scores, axis=0, keepdims=True)
    gates = RSCALE * scores / ssum
    small[0] = scores
    small[1] = gates
    small[2] = jnp.broadcast_to(ssum, scores.shape)
    gate_half = gates.astype(BF16).astype(F32)
    window = iota((NE, T), 0)
    mask = jnp.zeros((NE, T), F32)
    gate_e = jnp.zeros((NE, T), F32)
    for k, row in enumerate(k_rows):
        hit = window == row
        mask = jnp.where(hit, 1.0, mask)
        gate_e = jnp.where(hit, gate_half[k : k + 1, :], gate_e)
    earlier = (iota((T, T), 0) < iota((T, T), 1)).astype(F32).astype(BF16)
    rank = jnp.dot(mask.astype(BF16), earlier, preferred_element_type=F32)
    pos = jnp.where(mask > 0.0, rank, 255.0)
    posv[...] = pos
    lane = iota((NE, T), 1)
    slot_gates = jnp.zeros((NE, T), F32)
    for c in range(8):
        v = jnp.sum(jnp.where(pos == float(c), gate_e, 0.0), axis=1, keepdims=True)
        slot_gates = jnp.where(lane == c, v, slot_gates)
    gsend[...] = slot_gates[:, None, :]
    pos_half = pos.astype(BF16)

    pl.semaphore_wait(barrier, NE - 1 + (NDP - 1) * NY)

    own_w.wait()

    def w_rows(owner):
        return wfull.at[pl.ds(pl.multiple_of(owner * FS, FS), FS)]

    def tok_cols(yy):
        return tok.at[:, pl.ds(pl.multiple_of(yy * Q, 128), Q)]

    pair = (x * NC + 1 - core, e)
    for d in range(1, NX):
        remote(w_rows(dp), w_rows(dp), wx_s.at[d - 1], wx_r.at[d - 1], (lax.rem(x + d, NX) * NC + core, e)).start()
    remote(w_rows(dp), w_rows(dp), wc_s.at[0], wc_r.at[0], pair).start()
    for d in range(1, NY):
        yy = lax.rem(y + d, NY)
        remote(tok_cols(yy), tokg.at[dp, y], t1_s, t1_r, (dp, yy * NZ + z)).start()
    pltpu.make_async_copy(tok_cols(y), tokg.at[dp, y], t1_r).start()

    def order(i):
        half = (i + 1) // 2
        return lax.rem(m0 + NG // 2 + jnp.where(i % 2 == 1, NG - half, half), NG)

    def send_group(i, c):
        m = order(i)
        jj = iota((GS * 16, NE), 0) // 16
        ex = jj // 2 * NZ + 2 * m + jj % 2
        pick = (iota((GS * 16, NE), 1) == ex).astype(F32).astype(BF16)
        spread = jnp.dot(pick, pos_half, preferred_element_type=F32)
        row = iota((GS * 16, T), 0)
        table = (spread == (row % 8).astype(F32)).astype(F32).astype(BF16)
        first = iota((GS * 16, 1), 0) % 16 < 8
        a = jnp.dot(table, og[:, :H], preferred_element_type=F32)
        b = jnp.dot(table, og[:, H:], preferred_element_type=F32)
        send[m] = jnp.where(first, a, b).astype(BF16).reshape(GS, 16, H)

        def one(j, c2):
            to = j // 2 * NZ + 2 * m + j % 2

            @pl.when(to != e)
            def _():
                remote(send.at[m, j], recv.at[m0, y * 2 + z % 2], row_s, row_r.at[m0], (dp, to)).start()
                remote(gsend.at[to], grecv.at[place], gate_s, gate_r, (dp, to)).start()

            @pl.when(to == e)
            def _():
                pltpu.make_async_copy(send.at[m, j], recv.at[m, j], row_r.at[m]).start()
                pltpu.make_async_copy(gsend.at[e], grecv.at[place], gate_r).start()

            return c2

        return lax.fori_loop(0, GS, one, c)

    lax.fori_loop(0, NG, send_group, 0)

    for d in range(1, NX):
        shard = lax.rem(x + NX - d, NX) * NC + core
        remote(w_rows(shard), w_rows(shard), wx_s.at[d - 1], wx_r.at[d - 1], pair).wait_recv()
        remote(w_rows(shard), w_rows(shard), wc_s.at[d], wc_r.at[d], pair).start()
    drain(tokg.at[dp], t1_r)
    for d in range(1, NX):
        remote(tokg.at[dp], tokg.at[dp], tx_s.at[d - 1], tx_r.at[d - 1], (lax.rem(x + d, NX) * NC + core, e)).start()
    remote(tokg.at[dp], tokg.at[dp], tc_s.at[0], tc_r.at[0], pair).start()
    for d in range(NX):
        shard = lax.rem(x + NX - d, NX) * NC + 1 - core
        drain(w_rows(shard), wc_r.at[d])
    load.wait()
    drain(grecv, gate_r)

    lane8 = iota((GS, 8, 128), 2) == iota((GS, 8, 128), 1)
    FC = min(FW, 256)

    def work(i, c):
        m = order(i)
        drain(recv.at[m], row_r.at[m])
        rows = recv[m].reshape(GS * 16, H)
        gate_col = jnp.sum(
            jnp.where(lane8, grecv[pl.ds(pl.multiple_of(m * GS, GS), GS)], 0.0), axis=2, keepdims=True
        )
        span = pl.ds(pl.multiple_of(m * 16, 16), 16)
        back = jnp.zeros((GS, 8, 1), F32)
        nt = (((1,), (1,)), ((), ()))
        for f in range(0, FW, FC):
            a = lax.dot_general(rows, wfull[f : f + FC, :H], nt, preferred_element_type=F32)
            b = lax.dot_general(rows, wfull[f : f + FC, H:], nt, preferred_element_type=F32)
            g = a.reshape(GS, 16, FC)[:, :8] + b.reshape(GS, 16, FC)[:, 8:]
            hid[:, span, f : f + FC] = (gate_col * g).reshape(NY, 16, FC).astype(BF16)
            kept = savedv[:, span, f : f + FC].astype(F32).reshape(GS, 8, FC)
            back = back + jnp.sum(kept * g, axis=2, keepdims=True)
        rsend[pl.ds(pl.multiple_of(m * GS, GS), GS)] = jnp.sum(jnp.where(lane8, back, 0.0), axis=1, keepdims=True)

        def one(j, c2):
            to = j // 2 * NZ + 2 * m + j % 2

            @pl.when(to != e)
            def _():
                remote(rsend.at[m * GS + j], rrecv.at[e], ret_s, ret_r, (dp, to)).start()

            @pl.when(to == e)
            def _():
                pltpu.make_async_copy(rsend.at[m * GS + j], rrecv.at[e], ret_r).start()

            return c2

        return lax.fori_loop(0, GS, one, c)

    lax.fori_loop(0, NG // 2, work, 0)
    for d in range(1, NX):
        shard = lax.rem(x + NX - d, NX) * NC + core
        drain(tokg.at[shard], tx_r.at[d - 1])
        remote(tokg.at[shard], tokg.at[shard], tc_s.at[d], tc_r.at[d], pair).start()
    lax.fori_loop(NG // 2, NG, work, 0)
    for d in range(NX):
        shard = lax.rem(x + NX - d, NX) * NC + 1 - core
        drain(tokg.at[shard], tc_r.at[d])

    drain(rrecv, ret_r)
    ret = rrecv[...].reshape(NE, 128)
    pos = posv[...]
    grad_e = jnp.zeros((NE, T), F32)
    for c in range(8):
        grad_e = jnp.where(pos == float(c), ret[:, c : c + 1], grad_e)
    scores, gates, ssum = small[0], small[1], small[2]
    k_rows = [ids[k : k + 1, :] for k in range(ids.shape[0])]
    window = iota((NE, T), 0)
    choice = jnp.concatenate(
        [jnp.sum(jnp.where(window == row, grad_e, 0.0), axis=0, keepdims=True) for row in k_rows], axis=0
    )
    mixed = jnp.sum(choice * gates, axis=0, keepdims=True) / RSCALE
    dchosen = RSCALE / ssum * (choice - mixed) * scores * (1.0 - scores)
    names = iota((EX, T), 0)
    lgt = zterm[...]
    for k, row in enumerate(k_rows):
        lgt = lgt + jnp.where(names == row, dchosen[k : k + 1, :], 0.0)
    for d in range(NDP):
        lgs[d] = lgt[d * ED : (d + 1) * ED]

    mine = dp * NY + y

    def spread_lg(i, c):
        to_dp, to_y = lax.rem(dp + i // NY, NDP), lax.rem(y + i, NY)
        remote(lgs.at[to_dp], lgb.at[mine], lg_s, lg_r, (to_dp, to_y * NZ + z)).start()
        return c

    lax.fori_loop(1, NDP * NY, spread_lg, 0)
    pltpu.make_async_copy(lgs.at[dp], lgb.at[mine], lg_r).start()
    if EX > 128:
        lg[:, :128] = lgt[:128].T
        lg[:, 128:] = lgt[EX - 128 :].T[:, 256 - EX :]
    else:
        lg[...] = lgt.T
    drain(lgb, lg_r)
    for s in range(NDP * NY):
        v = lgb[s]
        hi = v.astype(BF16)
        lhs[:, s * T : (s + 1) * T] = jnp.concatenate([v, v - hi.astype(F32)], axis=0).astype(BF16)
    panel = jnp.zeros((2 * ED, Q), F32)
    for d in range(NDP):
        panel = panel + jnp.dot(
            lhs[:, d * NY * T : (d + 1) * NY * T], tokg[d].reshape(NY * T, Q), preferred_element_type=F32
        )
    panel = panel[:ED] + panel[ED:]
    for j in range(NZ):
        zsend[j, :, :R] = panel[:, j * R : (j + 1) * R]
        if R < 128:
            zsend[j, :, R:] = jnp.zeros((ED, 128 - R), F32)

    def spread_z(i, c):
        to = lax.rem(z + i, NZ)
        remote(zsend.at[to], zrecv.at[z], z_s, z_r, (dp, y * NZ + to)).start()
        return c

    lax.fori_loop(1, NZ, spread_z, 0)
    pltpu.make_async_copy(zsend.at[z], zrecv.at[z], z_r).start()
    drain(zrecv, z_r)
    out = zrecv[0]
    for j in range(1, NZ):
        out = out + zrecv[j]
    out = jnp.concatenate([out, jnp.zeros((128 - ED, 128), F32)], axis=0).T
    rg[...] = out[:R, :ED]

    drain(send.at[pl.ds(0, NG - 1)], row_s)
    drain(send.at[0, pl.ds(0, GS - 1)], row_s)
    drain(gsend.at[pl.ds(0, NE - 1)], gate_s)
    drain(rsend.at[pl.ds(0, NE - 1)], ret_s)
    for d in range(NX - 1):
        drain(w_rows(dp), wx_s.at[d])
        drain(tokg.at[dp], tx_s.at[d])
    for d in range(NX):
        drain(w_rows(dp), wc_s.at[d])
        drain(tokg.at[dp], tc_s.at[d])
    drain(tokg.at[dp, pl.ds(0, NY - 1)], t1_s)
    drain(lgb.at[pl.ds(0, NDP * NY - 1)], lg_s)
    drain(zsend.at[pl.ds(0, NZ - 1)], z_s)


def local(dims, tokens_in, out_grad, router_logits, expert_ids, saved_hidden, down_weight):
    NX, NY, NZ = dims
    NDP, NE, NG, GS = NX * NC, NY * NZ, NZ // 2, NY * 2
    T, D = out_grad.shape
    FW = saved_hidden.shape[4]
    EX = router_logits.shape[1]
    ED, Q, R = EX // NDP, D // NY, D // NE
    vmem = pl.BlockSpec(memory_space=pltpu.VMEM)
    hbm = pl.BlockSpec(memory_space=pl.ANY)
    dma = pltpu.SemaphoreType.DMA
    one = dma(())
    hid, lg, rg = pl.pallas_call(
        functools.partial(kernel, dims),
        out_shape=(
            jax.ShapeDtypeStruct((NY, NZ * 8, FW), BF16),
            jax.ShapeDtypeStruct((T, EX), F32),
            jax.ShapeDtypeStruct((R, ED), F32),
        ),
        in_specs=[vmem, vmem, vmem, hbm, hbm, hbm],
        out_specs=(vmem, vmem, vmem),
        scratch_shapes=[
            pltpu.VMEM((NG, GS, 16, D // 2), BF16),
            pltpu.VMEM((NG, GS, 16, D // 2), BF16),
            pltpu.VMEM((FW, D), BF16),
            pltpu.VMEM((NDP, NY, T, Q), BF16),
            pltpu.VMEM((NY, NZ * 8, FW), BF16),
            pltpu.VMEM((NE, 1, 128), F32),
            pltpu.VMEM((NE, 1, 128), F32),
            pltpu.VMEM((NE, 1, 128), F32),
            pltpu.VMEM((NE, 1, 128), F32),
            pltpu.VMEM((NDP, ED, T), F32),
            pltpu.VMEM((NDP * NY, ED, T), F32),
            pltpu.VMEM((2 * ED, NDP * NY * T), BF16),
            pltpu.VMEM((NZ, ED, 128), F32),
            pltpu.VMEM((NZ, ED, 128), F32),
            pltpu.VMEM((EX, T), F32),
            pltpu.VMEM((NE, T), F32),
            pltpu.VMEM((3, 8, T), F32),
            dma((NG,)), one, one, one, one, one,
            dma((NX - 1,)), dma((NX - 1,)), dma((NX,)), dma((NX,)),
            one, one, dma((NX - 1,)), dma((NX - 1,)), dma((NX,)), dma((NX,)),
            one, one, one, one, dma((2,)),
        ],
        compiler_params=pltpu.CompilerParams(
            collective_id=0, has_side_effects=True, vmem_limit_bytes=56 * 2**20
        ),
        cost_estimate=pl.CostEstimate(flops=4 * 10**9, bytes_accessed=6 * 10**6, transcendentals=0),
    )(
        out_grad,
        router_logits,
        expert_ids.T,
        tokens_in,
        down_weight.reshape(FW // NDP, D),
        saved_hidden.reshape(NY, NZ * 8, FW),
    )
    return hid.reshape(1, 1, NE, 8, FW), lg, rg


def solution(mesh, dims=(4, 4, 16)):
    in_specs = (
        P(("dp", "expert"), None),
        P(("dp", "expert"), None),
        P(("dp", "expert"), None),
        P(("dp", "expert"), None),
        P("dp", "expert", None, None, None),
        P("expert", "dp", None),
    )
    out_specs = (P("dp", "expert", None, None, None), P(("dp", "expert"), None), P("expert", "dp"))
    return jax.shard_map(
        functools.partial(local, dims), mesh=mesh, in_specs=in_specs, out_specs=out_specs, check_vma=False
    )
```

```python
import functools

import jax
import jax.numpy as jnp
from jax import lax
from jax.experimental import pallas as pl
from jax.experimental.pallas import tpu as pltpu
from jax.sharding import PartitionSpec as P

RSCALE = 2.827
ZLOSS = 0.25
NC = 2
MESH = pl.DeviceIdType.MESH
F32 = jnp.float32
BF16 = jnp.bfloat16


def drain(ref, sem):
    pltpu.make_async_copy(ref, ref, sem).wait()


def iota(shape, dim):
    return lax.broadcasted_iota(jnp.int32, shape, dim)


def kernel(
    dims,
    og, logits, ids, tok, w, saved,
    hid, lg, rg,
    ring, meta, nsend, nrecv, fsend, frecv, ftable, gnsend, gnrecv, gfsend, gfrecv, half,
    wfull, tokg, savedv, savedf, hidf, rsend, rrecv, lgb, lhs, zsend, zrecv, zterm, posv, small,
    ring_s, ring_r, meta_s, meta_r, near_s, near_r, gn_s, gn_r, far_s, far_r, gf_s, gf_r, ret_s, ret_r,
    wx_s, wx_r, wc_s, wc_r, t1_s, t1_r, tx_s, tx_r, tc_s, tc_r, lg_s, lg_r, z_s, z_r, local_sem,
):
    NX, NY, NZ = dims
    NDP, NE = NX * NC, NY * NZ
    RE = NZ // 4
    NN, NF = 2 * RE + 1, 2 * RE - 1
    T, D = og.shape
    H = D // 2
    Q = D // NY
    FW = wfull.shape[0]
    FS = FW // NDP
    FC = min(FW, 256)
    EX = logits.shape[0]
    ED = EX // NDP
    R = D // NE
    dp, e = lax.axis_index("dp"), lax.axis_index("expert")
    x, core = dp // NC, dp % NC
    y, z = e // NZ, e % NZ
    nt = (((1,), (1,)), ((), ()))

    def remote(src, dst, s, r, dev):
        return pltpu.make_async_remote_copy(
            src_ref=src, dst_ref=dst, send_sem=s, recv_sem=r, device_id=dev, device_id_type=MESH
        )

    barrier = pltpu.get_barrier_semaphore()

    def greet(i, c):
        pl.semaphore_signal(barrier, inc=1, device_id=(dp, lax.rem(e + i, NE)), device_id_type=MESH)
        return c

    lax.fori_loop(1, NE, greet, 0)

    def greet2(i, c):
        other = lax.rem(dp + 1 + i // NY, NDP)
        pl.semaphore_signal(barrier, inc=1, device_id=(other, lax.rem(i, NY) * NZ + z), device_id_type=MESH)
        return c

    lax.fori_loop(0, (NDP - 1) * NY, greet2, 0)
    load = pltpu.make_async_copy(saved, savedv, local_sem.at[0])
    load.start()
    own_w = pltpu.make_async_copy(w, wfull.at[pl.ds(pl.multiple_of(dp * FS, FS), FS)], local_sem.at[1])
    own_w.start()

    lt = logits[...]
    top = jnp.max(lt, axis=0, keepdims=True)
    shifted = jnp.exp(lt - top)
    total = jnp.sum(shifted, axis=0, keepdims=True)
    lse = top + jnp.log(total)
    zterm[...] = (2.0 * ZLOSS) * lse * (shifted / total)
    names = iota((EX, T), 0)
    k_rows = [ids[k : k + 1, :] for k in range(8)]
    chosen = jnp.concatenate(
        [jnp.sum(jnp.where(names == row, lt, 0.0), axis=0, keepdims=True) for row in k_rows], axis=0
    )
    scores = 1.0 / (1.0 + jnp.exp(-chosen))
    ssum = jnp.sum(scores, axis=0, keepdims=True)
    gates = RSCALE * scores / ssum
    small[0] = scores
    small[1] = gates
    small[2] = jnp.broadcast_to(ssum, scores.shape)
    own_meta = meta.at[2 * RE]
    own_meta[0:8] = ids[...].astype(F32)
    own_meta[8:16] = gates.astype(BF16).astype(F32)
    lane8 = iota((NY, 8, 128), 2) == iota((NY, 8, 128), 1)

    def slots(info):
        window = iota((NE, T), 0).astype(F32)
        mask = jnp.zeros((NE, T), F32)
        gate = jnp.zeros((NE, T), F32)
        for k in range(8):
            hit = window == info[k : k + 1, :]
            mask = jnp.where(hit, 1.0, mask)
            gate = jnp.where(hit, info[8 + k : 9 + k, :], gate)
        earlier = (iota((T, T), 0) < iota((T, T), 1)).astype(F32).astype(BF16)
        rank = jnp.dot(mask.astype(BF16), earlier, preferred_element_type=F32)
        return jnp.where(mask > 0.0, rank, 255.0), gate

    def tables(pos, gate, experts):
        n = experts.shape[0]
        pick = (iota((n, NE), 1) == experts).astype(F32).astype(BF16)
        spread = jnp.dot(pick, pos.astype(BF16), preferred_element_type=F32)
        hit = spread == (iota((n, T), 0) % 8).astype(F32)
        gates_at = jnp.dot(pick, gate.astype(BF16), preferred_element_type=F32)
        col = jnp.sum(jnp.where(hit, gates_at, 0.0), axis=1, keepdims=True).reshape(n // 8, 8, 1)
        at = iota((n // 8, 8, 128), 2) == iota((n // 8, 8, 128), 1)
        return hit.astype(F32).astype(BF16), jnp.sum(jnp.where(at, col, 0.0), axis=1, keepdims=True)

    def dispatch(ni, low, high, pos, gate):
        experts = iota((NY * 8, 1), 0) // 8 * NZ + z
        table, rows = tables(pos, gate, experts)
        gnsend[ni] = rows
        a = jnp.dot(table, low, preferred_element_type=F32).reshape(NY, 8, H)
        b = jnp.dot(table, high, preferred_element_type=F32).reshape(NY, 8, H)
        nsend[ni] = jnp.concatenate([a, b], axis=1).astype(BF16)
        for d in range(1, NY):
            yy = lax.rem(y + d, NY)
            remote(nsend.at[ni, yy], nrecv.at[ni, y], near_s, near_r.at[ni], (dp, yy * NZ + z)).start()
            remote(gnsend.at[ni, yy], gnrecv.at[ni, y], gn_s, gn_r.at[ni], (dp, yy * NZ + z)).start()
        pltpu.make_async_copy(nsend.at[ni, y], nrecv.at[ni, y], near_r.at[ni]).start()
        pltpu.make_async_copy(gnsend.at[ni, y], gnrecv.at[ni, y], gn_r.at[ni]).start()

    def hop(g, st, c):
        to = (dp, y * NZ + lax.rem(z + (1 if g == 0 else NZ - 1), NZ))
        src = og.at[:, pl.ds(c * H, H)] if st == 0 else ring.at[g, st - 1, c]
        remote(src, ring.at[g, st, c], ring_s.at[g, st, c], ring_r.at[g, st, c], to).start()
        if c == 0:
            info = own_meta if st == 0 else meta.at[g * RE + st - 1]
            remote(info, meta.at[g * RE + st], meta_s.at[g, st], meta_r.at[g, st], to).start()

    def arrived(g, st, c):
        if c == 0:
            drain(meta.at[g * RE + st], meta_r.at[g, st])
        drain(ring.at[g, st, c], ring_r.at[g, st, c])

    def relay(g, c):
        n = RE * NY
        if c == 0:
            d = iota((n * 8, 1), 0) // 8
            step = d // NY + 1
            experts = (y + d % NY) % NY * NZ + (z + (step if g == 0 else NZ - step)) % NZ
            pos, gate = slots(meta[g * RE + RE - 1])
            table, rows = tables(pos, gate, experts)
            ftable[g] = table
            gfsend[g] = rows
        p = jnp.dot(ftable[g], ring[g, RE - 1, c], preferred_element_type=F32).reshape(n, 8, H)
        fsend[c, g] = jnp.concatenate([p[:, :, : H // 2], p[:, :, H // 2 :]], axis=1).astype(BF16)

        def one(d, carry):
            j = d // NY + 1
            to = (dp, lax.rem(y + d % NY, NY) * NZ + lax.rem(z + (j if g == 0 else NZ - j), NZ))
            fi = j - 1 if g == 0 else jnp.where(j == RE, RE - 1, RE - 1 + j)
            remote(fsend.at[c, g, d], frecv.at[c, fi, y], far_s, far_r.at[c], to).start()
            if c == 0:
                remote(gfsend.at[g, d], gfrecv.at[fi, y], gf_s, gf_r, to).start()
            return carry

        last = (RE - 1) * NY
        split = last + NY // 2
        lax.fori_loop(*((last, split) if g == 0 else (split, RE * NY)), one, 0)
        lax.fori_loop(0, last, one, 0)

    def w_rows(owner):
        return wfull.at[pl.ds(pl.multiple_of(owner * FS, FS), FS)]

    def tok_cols(yy):
        return tok.at[:, pl.ds(pl.multiple_of(yy * Q, 128), Q)]

    pair = (x * NC + 1 - core, e)
    own_w.wait()
    pl.semaphore_wait(barrier, NE - 1 + (NDP - 1) * NY)

    for c in range(2):
        for g in range(2):
            hop(g, 0, c)
    for d in range(1, NX):
        remote(w_rows(dp), w_rows(dp), wx_s.at[d - 1], wx_r.at[d - 1], (lax.rem(x + d, NX) * NC + core, e)).start()
    remote(w_rows(dp), w_rows(dp), wc_s.at[0], wc_r.at[0], pair).start()
    for d in range(1, NY):
        yy = lax.rem(y + d, NY)
        remote(tok_cols(yy), tokg.at[dp, y], t1_s, t1_r, (dp, yy * NZ + z)).start()
    pltpu.make_async_copy(tok_cols(y), tokg.at[dp, y], t1_r).start()

    pos, gate = slots(own_meta[...])
    posv[...] = pos
    dispatch(0, og[:, :H], og[:, H:], pos, gate)
    load.wait()
    savedf[...] = savedv[...].astype(F32).reshape(NY, NZ, 8, FW)

    for st in range(1, RE):
        for c in range(2):
            for g in range(2):
                arrived(g, st - 1, c)
                hop(g, st, c)
        for g in range(2):
            pos, gate = slots(meta[g * RE + st - 1])
            dispatch(2 * st - 1 + g, ring[g, st - 1, 0], ring[g, st - 1, 1], pos, gate)
        if st == max(RE - 2, 1):
            for d in range(1, NX):
                shard = lax.rem(x + NX - d, NX) * NC + core
                drain(w_rows(shard), wx_r.at[d - 1])
                remote(w_rows(shard), w_rows(shard), wc_s.at[d], wc_r.at[d], pair).start()
            drain(tokg.at[dp], t1_r)
            for d in range(1, NX):
                to = (lax.rem(x + d, NX) * NC + core, e)
                remote(tokg.at[dp], tokg.at[dp], tx_s.at[d - 1], tx_r.at[d - 1], to).start()
            remote(tokg.at[dp], tokg.at[dp], tc_s.at[0], tc_r.at[0], pair).start()

    def joined(block, n, width):
        v = block.astype(F32)
        low = v[:, :8].reshape(n * 8, width)
        high = v[:, 8:].reshape(n * 8, width)
        return jnp.concatenate([low, high], axis=1).astype(BF16)

    def finish(f, g, backs, columns, sources):
        for i, zs in enumerate(sources):
            part = g[i * NY * 8 : (i + 1) * NY * 8].reshape(NY, 8, FC)
            hidf[:, zs, :, f : f + FC] = columns[i] * part
            backs[i] = backs[i] + jnp.sum(savedf[:, zs, :, f : f + FC] * part, axis=2, keepdims=True)

    def column(rows):
        return jnp.sum(jnp.where(lane8, rows, 0.0), axis=2, keepdims=True)

    def give_back(i, zs, back):
        rsend[i] = jnp.sum(jnp.where(lane8, back, 0.0), axis=1, keepdims=True)
        for d in range(NY):
            yy = lax.rem(y + d, NY)
            if i == 0 and d == 0:
                pltpu.make_async_copy(rsend.at[i, yy], rrecv.at[e], ret_r).start()
            else:
                remote(rsend.at[i, yy], rrecv.at[e], ret_s, ret_r, (dp, yy * NZ + zs)).start()

    def near(group):
        sources = []
        for ni in group:
            drain(nrecv.at[ni], near_r.at[ni])
            drain(gnrecv.at[ni], gn_r.at[ni])
            st = (ni + 1) // 2
            sources.append(lax.rem(z + (NZ - st if ni % 2 == 1 else st), NZ))
        rows = jnp.concatenate([joined(nrecv[ni], NY, H) for ni in group], axis=0)
        columns = [column(gnrecv[ni]) for ni in group]
        backs = [jnp.zeros((NY, 8, 1), F32) for ni in group]
        for f in range(0, FW, FC):
            g = lax.dot_general(rows, wfull[f : f + FC], nt, preferred_element_type=F32)
            finish(f, g, backs, columns, sources)
        for ni, zs, back in zip(group, sources, backs):
            give_back(ni, zs, back)

    for c in range(2):
        for g in range(2):
            arrived(g, RE - 1, c)
            relay(g, c)
    for g in range(2):
        pos, gate = slots(meta[g * RE + RE - 1])
        dispatch(2 * RE - 1 + g, ring[g, RE - 1, 0], ring[g, RE - 1, 1], pos, gate)
    for d in range(NX):
        shard = lax.rem(x + NX - d, NX) * NC + 1 - core
        drain(w_rows(shard), wc_r.at[d])
    near([0, 1, 2])
    for first in range(3, NN, 4):
        near(list(range(first, min(first + 4, NN))))
    for d in range(1, NX):
        shard = lax.rem(x + NX - d, NX) * NC + core
        drain(tokg.at[shard], tx_r.at[d - 1])
        remote(tokg.at[shard], tokg.at[shard], tc_s.at[d], tc_r.at[d], pair).start()

    drain(frecv.at[0], far_r.at[0])
    rows = joined(frecv[0].reshape(NF * NY, 16, H // 2), NF * NY, H // 2)
    for f in range(0, FW, FC):
        half[:, f : f + FC] = lax.dot_general(rows, wfull[f : f + FC, :H], nt, preferred_element_type=F32)
    drain(gfrecv, gf_r)
    columns = [column(gfrecv[i]) for i in range(NF)]
    backs = [jnp.zeros((NY, 8, 1), F32) for i in range(NF)]
    sources = [lax.rem(z + (NZ - RE - 1 - i if i < RE else i + 1), NZ) for i in range(NF)]
    drain(frecv.at[1], far_r.at[1])
    rows = joined(frecv[1].reshape(NF * NY, 16, H // 2), NF * NY, H // 2)
    for f in range(0, FW, FC):
        g = lax.dot_general(rows, wfull[f : f + FC, H:], nt, preferred_element_type=F32)
        finish(f, g + half[:, f : f + FC], backs, columns, sources)
    for i in range(NF):
        give_back(NN + i, sources[i], backs[i])
    hid[...] = hidf[...].reshape(NY, NZ * 8, FW).astype(BF16)
    for d in range(NX):
        shard = lax.rem(x + NX - d, NX) * NC + 1 - core
        drain(tokg.at[shard], tc_r.at[d])

    drain(rrecv, ret_r)
    ret = rrecv[...].reshape(NE, 128)
    pos = posv[...]
    grad_e = jnp.zeros((NE, T), F32)
    for c in range(8):
        grad_e = jnp.where(pos == float(c), ret[:, c : c + 1], grad_e)
    scores, gates, ssum = small[0], small[1], small[2]
    k_rows = [ids[k : k + 1, :] for k in range(8)]
    window = iota((NE, T), 0)
    choice = jnp.concatenate(
        [jnp.sum(jnp.where(window == row, grad_e, 0.0), axis=0, keepdims=True) for row in k_rows], axis=0
    )
    mixed = jnp.sum(choice * gates, axis=0, keepdims=True) / RSCALE
    dchosen = RSCALE / ssum * (choice - mixed) * scores * (1.0 - scores)
    names = iota((EX, T), 0)
    lgt = zterm[...]
    for k, row in enumerate(k_rows):
        lgt = lgt + jnp.where(names == row, dchosen[k : k + 1, :], 0.0)
    lg[...] = lgt.reshape(NDP, ED, T)

    mine = dp * NY + y

    def spread_lg(i, c):
        to_dp, to_y = lax.rem(dp + i // NY, NDP), lax.rem(y + i, NY)
        remote(lg.at[to_dp], lgb.at[mine], lg_s, lg_r, (to_dp, to_y * NZ + z)).start()
        return c

    lax.fori_loop(1, NDP * NY, spread_lg, 0)
    pltpu.make_async_copy(lg.at[dp], lgb.at[mine], lg_r).start()
    drain(lgb, lg_r)
    for s in range(NDP * NY):
        v = lgb[s]
        hi = v.astype(BF16)
        lhs[:, s * T : (s + 1) * T] = jnp.concatenate([v, v - hi.astype(F32)], axis=0).astype(BF16)
    panel = jnp.zeros((2 * ED, Q), F32)
    for d in range(NDP):
        panel = panel + jnp.dot(
            lhs[:, d * NY * T : (d + 1) * NY * T], tokg[d].reshape(NY * T, Q), preferred_element_type=F32
        )
    panel = panel[:ED] + panel[ED:]
    for j in range(NZ):
        zsend[j, :, :R] = panel[:, j * R : (j + 1) * R]
        if R < 128:
            zsend[j, :, R:] = jnp.zeros((ED, 128 - R), F32)

    def spread_z(i, c):
        to = lax.rem(z + i, NZ)
        remote(zsend.at[to], zrecv.at[z], z_s, z_r, (dp, y * NZ + to)).start()
        return c

    lax.fori_loop(1, NZ, spread_z, 0)
    pltpu.make_async_copy(zsend.at[z], zrecv.at[z], z_r).start()
    drain(zrecv, z_r)
    out = zrecv[0]
    for j in range(1, NZ):
        out = out + zrecv[j]
    rg[...] = out[:, :R]

    for g in range(2):
        for st in range(RE):
            drain(meta.at[0], meta_s.at[g, st])
            for c in range(2):
                drain(ring.at[0, 0, 0], ring_s.at[g, st, c])
    drain(nsend.at[:, pl.ds(0, NY - 1)], near_s)
    drain(gnsend.at[:, pl.ds(0, NY - 1)], gn_s)
    drain(frecv, far_s)
    drain(gfrecv, gf_s)
    drain(rsend.at[pl.ds(1, NZ - 1)], ret_s)
    drain(rsend.at[0, pl.ds(0, NY - 1)], ret_s)
    for d in range(NX - 1):
        drain(w_rows(dp), wx_s.at[d])
        drain(tokg.at[dp], tx_s.at[d])
    for d in range(NX):
        drain(w_rows(dp), wc_s.at[d])
        drain(tokg.at[dp], tc_s.at[d])
    drain(tokg.at[dp, pl.ds(0, NY - 1)], t1_s)
    drain(lgb.at[pl.ds(0, NDP * NY - 1)], lg_s)
    drain(zsend.at[pl.ds(0, NZ - 1)], z_s)


def local(dims, tokens_in, out_grad, router_logits, expert_ids, saved_hidden, down_weight):
    NX, NY, NZ = dims
    NDP, NE = NX * NC, NY * NZ
    RE = NZ // 4
    NN, NF = 2 * RE + 1, 2 * RE - 1
    T, D = out_grad.shape
    H = D // 2
    FW = saved_hidden.shape[4]
    EX = router_logits.shape[1]
    ED, Q, R = EX // NDP, D // NY, D // NE
    vmem = pl.BlockSpec(memory_space=pltpu.VMEM)
    hbm = pl.BlockSpec(memory_space=pl.ANY)
    dma = pltpu.SemaphoreType.DMA
    one = dma(())
    hid, lg, rg = pl.pallas_call(
        functools.partial(kernel, dims),
        out_shape=(
            jax.ShapeDtypeStruct((NY, NZ * 8, FW), BF16),
            jax.ShapeDtypeStruct((NDP, ED, T), F32),
            jax.ShapeDtypeStruct((ED, R), F32),
        ),
        in_specs=[vmem, vmem, vmem, hbm, hbm, hbm],
        out_specs=(vmem, vmem, vmem),
        scratch_shapes=[
            pltpu.VMEM((2, RE, 2, T, H), BF16),
            pltpu.VMEM((2 * RE + 1, 16, T), F32),
            pltpu.VMEM((NN, NY, 16, H), BF16),
            pltpu.VMEM((NN, NY, 16, H), BF16),
            pltpu.VMEM((2, 2, RE * NY, 16, H // 2), BF16),
            pltpu.VMEM((2, NF, NY, 16, H // 2), BF16),
            pltpu.VMEM((2, RE * NY * 8, T), BF16),
            pltpu.VMEM((NN, NY, 1, 128), F32),
            pltpu.VMEM((NN, NY, 1, 128), F32),
            pltpu.VMEM((2, RE * NY, 1, 128), F32),
            pltpu.VMEM((NF, NY, 1, 128), F32),
            pltpu.VMEM((NF * NY * 8, FW), F32),
            pltpu.VMEM((FW, D), BF16),
            pltpu.VMEM((NDP, NY, T, Q), BF16),
            pltpu.VMEM((NY, NZ * 8, FW), BF16),
            pltpu.VMEM((NY, NZ, 8, FW), F32),
            pltpu.VMEM((NY, NZ, 8, FW), F32),
            pltpu.VMEM((NZ, NY, 1, 128), F32),
            pltpu.VMEM((NE, 1, 128), F32),
            pltpu.VMEM((NDP * NY, ED, T), F32),
            pltpu.VMEM((2 * ED, NDP * NY * T), BF16),
            pltpu.VMEM((NZ, ED, 128), F32),
            pltpu.VMEM((NZ, ED, 128), F32),
            pltpu.VMEM((EX, T), F32),
            pltpu.VMEM((NE, T), F32),
            pltpu.VMEM((3, 8, T), F32),
            dma((2, RE, 2)), dma((2, RE, 2)), dma((2, RE)), dma((2, RE)),
            one, dma((NN,)), one, dma((NN,)), one, dma((2,)), one, one, one, one,
            dma((NX - 1,)), dma((NX - 1,)), dma((NX,)), dma((NX,)),
            one, one, dma((NX - 1,)), dma((NX - 1,)), dma((NX,)), dma((NX,)),
            one, one, one, one, dma((2,)),
        ],
        compiler_params=pltpu.CompilerParams(
            collective_id=0, has_side_effects=True, vmem_limit_bytes=58 * 2**20
        ),
        cost_estimate=pl.CostEstimate(flops=4 * 10**9, bytes_accessed=6 * 10**6, transcendentals=0),
    )(
        out_grad,
        router_logits.T,
        expert_ids.T,
        tokens_in,
        down_weight.reshape(FW // NDP, D),
        saved_hidden.reshape(NY, NZ * 8, FW),
    )
    return hid.reshape(1, 1, NE, 8, FW), lg.reshape(EX, T).T, rg.T


def solution(mesh, dims=(4, 4, 16)):
    in_specs = (
        P(("dp", "expert"), None),
        P(("dp", "expert"), None),
        P(("dp", "expert"), None),
        P(("dp", "expert"), None),
        P("dp", "expert", None, None, None),
        P("expert", "dp", None),
    )
    out_specs = (P("dp", "expert", None, None, None), P(("dp", "expert"), None), P("expert", "dp"))
    return jax.shard_map(
        functools.partial(local, dims), mesh=mesh, in_specs=in_specs, out_specs=out_specs, check_vma=False
    )
```

```python
import functools

import jax
import jax.numpy as jnp
from jax import lax
from jax.experimental import pallas as pl
from jax.experimental.pallas import tpu as pltpu
from jax.sharding import PartitionSpec as P

RSCALE = 2.827
ZLOSS = 0.25
NC = 2
MESH = pl.DeviceIdType.MESH
F32 = jnp.float32
BF16 = jnp.bfloat16


def drain(ref, sem):
    pltpu.make_async_copy(ref, ref, sem).wait()


def iota(shape, dim):
    return lax.broadcasted_iota(jnp.int32, shape, dim)


def kernel(
    dims,
    og_in, logits_in, ids_in, tok, w, saved,
    hid, lg, rg,
    ring, meta, nsend, nrecv, fsend, frecv, ftable, gnsend, gnrecv, gfsend, gfrecv, half,
    wfull, tokg, savedv, savedf, hidf, rsend, rrecv, esend, erecv, dsend, drecv, zsend, zrecv, zterm, posv, small, og, logits, ids,
    ring_s, ring_r, meta_s, meta_r, near_s, near_r, gn_s, gn_r, far_s, far_r, gf_s, gf_r, ret_s, ret_r,
    wx_s, wx_r, wc_s, wc_r, t1_s, t1_r, tx_s, tx_r, tc_s, tc_r, e_s, e_r, d_s, d_r, z_s, z_r, local_sem,
):
    NX, NY, NZ = dims
    NDP, NE = NX * NC, NY * NZ
    RE = NZ // 4
    NN, NF = 2 * RE + 1, 2 * RE - 1
    T, D = og_in.shape
    H = D // 2
    Q = D // NY
    FW = wfull.shape[0]
    FS = FW // NDP
    FC = min(FW, 256)
    EX = logits_in.shape[0]
    ED = EX // NDP
    R = D // NE
    dp, e = lax.axis_index("dp"), lax.axis_index("expert")
    x, core = dp // NC, dp % NC
    y, z = e // NZ, e % NZ
    nt = (((1,), (1,)), ((), ()))

    def remote(src, dst, s, r, dev):
        return pltpu.make_async_remote_copy(
            src_ref=src, dst_ref=dst, send_sem=s, recv_sem=r, device_id=dev, device_id_type=MESH
        )

    loads = [
        pltpu.make_async_copy(src, dst, local_sem.at[2 + i])
        for i, (src, dst) in enumerate(((logits_in, logits), (ids_in, ids), (og_in, og)))
    ]
    for copy in loads:
        copy.start()

    barrier = pltpu.get_barrier_semaphore()

    def greet(i, c):
        pl.semaphore_signal(barrier, inc=1, device_id=(dp, lax.rem(e + i, NE)), device_id_type=MESH)
        return c

    lax.fori_loop(1, NE, greet, 0)

    def greet2(i, c):
        other = lax.rem(dp + 1 + i // NY, NDP)
        pl.semaphore_signal(barrier, inc=1, device_id=(other, lax.rem(i, NY) * NZ + z), device_id_type=MESH)
        return c

    lax.fori_loop(0, (NDP - 1) * NY, greet2, 0)
    load = pltpu.make_async_copy(saved, savedv, local_sem.at[0])
    load.start()
    own_w = pltpu.make_async_copy(w, wfull.at[pl.ds(pl.multiple_of(dp * FS, FS), FS)], local_sem.at[1])
    own_w.start()

    loads[0].wait()
    loads[1].wait()
    lt = logits[...]
    top = jnp.max(lt, axis=0, keepdims=True)
    shifted = jnp.exp(lt - top)
    total = jnp.sum(shifted, axis=0, keepdims=True)
    lse = top + jnp.log(total)
    zterm[...] = (2.0 * ZLOSS) * lse * (shifted / total)
    names = iota((EX, T), 0)
    k_rows = [ids[k : k + 1, :] for k in range(8)]
    chosen = jnp.concatenate(
        [jnp.sum(jnp.where(names == row, lt, 0.0), axis=0, keepdims=True) for row in k_rows], axis=0
    )
    scores = 1.0 / (1.0 + jnp.exp(-chosen))
    ssum = jnp.sum(scores, axis=0, keepdims=True)
    gates = RSCALE * scores / ssum
    small[0] = scores
    small[1] = gates
    small[2] = jnp.broadcast_to(ssum, scores.shape)
    own_meta = meta.at[2 * RE]
    names_f = ids[...].astype(F32)
    own_meta[...] = jnp.concatenate([names_f, gates], axis=0).astype(BF16)
    for d in range(NDP):
        esend[d, :ED] = zterm[d * ED : (d + 1) * ED]
        esend[d, ED:] = names_f
    loads[2].wait()
    lane8 = iota((NY, 8, 128), 2) == iota((NY, 8, 128), 1)

    def slots(info):
        info = info.astype(F32)
        window = iota((NE, T), 0).astype(F32)
        mask = jnp.zeros((NE, T), F32)
        gate = jnp.zeros((NE, T), F32)
        for k in range(8):
            hit = window == info[k : k + 1, :]
            mask = jnp.where(hit, 1.0, mask)
            gate = jnp.where(hit, info[8 + k : 9 + k, :], gate)
        earlier = (iota((T, T), 0) < iota((T, T), 1)).astype(F32).astype(BF16)
        rank = jnp.dot(mask.astype(BF16), earlier, preferred_element_type=F32)
        return jnp.where(mask > 0.0, rank, 255.0), gate

    def tables(pos, gate, experts):
        n = experts.shape[0]
        pick = (iota((n, NE), 1) == experts).astype(F32).astype(BF16)
        spread = jnp.dot(pick, pos.astype(BF16), preferred_element_type=F32)
        hit = spread == (iota((n, T), 0) % 8).astype(F32)
        gates_at = jnp.dot(pick, gate.astype(BF16), preferred_element_type=F32)
        col = jnp.sum(jnp.where(hit, gates_at, 0.0), axis=1, keepdims=True).reshape(n // 8, 8, 1)
        at = iota((n // 8, 8, 128), 2) == iota((n // 8, 8, 128), 1)
        return hit.astype(F32).astype(BF16), jnp.sum(jnp.where(at, col, 0.0), axis=1, keepdims=True)

    def dispatch(ni, low, high, pos, gate):
        experts = iota((NY * 8, 1), 0) // 8 * NZ + z
        table, rows = tables(pos, gate, experts)
        gnsend[ni] = rows
        a = jnp.dot(table, low, preferred_element_type=F32).reshape(NY, 8, H)
        b = jnp.dot(table, high, preferred_element_type=F32).reshape(NY, 8, H)
        nsend[ni] = jnp.concatenate([a, b], axis=1).astype(BF16)
        for d in range(1, NY):
            yy = lax.rem(y + d, NY)
            remote(nsend.at[ni, yy], nrecv.at[ni, y], near_s, near_r.at[ni], (dp, yy * NZ + z)).start()
            remote(gnsend.at[ni, yy], gnrecv.at[ni, y], gn_s, gn_r.at[ni], (dp, yy * NZ + z)).start()
        pltpu.make_async_copy(nsend.at[ni, y], nrecv.at[ni, y], near_r.at[ni]).start()
        pltpu.make_async_copy(gnsend.at[ni, y], gnrecv.at[ni, y], gn_r.at[ni]).start()

    def hop(g, st, c):
        to = (dp, y * NZ + lax.rem(z + (1 if g == 0 else NZ - 1), NZ))
        src = og.at[:, pl.ds(c * H, H)] if st == 0 else ring.at[g, st - 1, c]
        remote(src, ring.at[g, st, c], ring_s.at[g, st, c], ring_r.at[g, st, c], to).start()
        if c == 0:
            info = own_meta if st == 0 else meta.at[g * RE + st - 1]
            remote(info, meta.at[g * RE + st], meta_s.at[g, st], meta_r.at[g, st], to).start()

    def arrived(g, st, c):
        if c == 0:
            drain(meta.at[g * RE + st], meta_r.at[g, st])
        drain(ring.at[g, st, c], ring_r.at[g, st, c])

    def relay(g, c):
        n = RE * NY
        if c == 0:
            d = iota((n * 8, 1), 0) // 8
            step = d // NY + 1
            experts = (y + d % NY) % NY * NZ + (z + (step if g == 0 else NZ - step)) % NZ
            pos, gate = slots(meta[g * RE + RE - 1])
            table, rows = tables(pos, gate, experts)
            ftable[g] = table
            gfsend[g] = rows
        p = jnp.dot(ftable[g], ring[g, RE - 1, c], preferred_element_type=F32).reshape(n, 8, H)
        fsend[c, g] = jnp.concatenate([p[:, :, : H // 2], p[:, :, H // 2 :]], axis=1).astype(BF16)

        def one(d, carry):
            j = d // NY + 1
            to = (dp, lax.rem(y + d % NY, NY) * NZ + lax.rem(z + (j if g == 0 else NZ - j), NZ))
            fi = j - 1 if g == 0 else jnp.where(j == RE, RE - 1, RE - 1 + j)
            remote(fsend.at[c, g, d], frecv.at[c, fi, y], far_s, far_r.at[c], to).start()
            if c == 0:
                remote(gfsend.at[g, d], gfrecv.at[fi, y], gf_s, gf_r, to).start()
            return carry

        last = (RE - 1) * NY
        split = last + NY // 2
        lax.fori_loop(*((last, split) if g == 0 else (split, RE * NY)), one, 0)
        lax.fori_loop(0, last, lambda i, carry: one(last - 1 - i, carry), 0)

    def w_rows(owner):
        return wfull.at[pl.ds(pl.multiple_of(owner * FS, FS), FS)]

    def tok_cols(yy):
        return tok.at[:, pl.ds(pl.multiple_of(yy * Q, 128), Q)]

    pair = (x * NC + 1 - core, e)
    own_w.wait()
    pl.semaphore_wait(barrier, NE - 1 + (NDP - 1) * NY)

    for c in range(2):
        for g in range(2):
            hop(g, 0, c)
    for d in range(1, NX):
        remote(w_rows(dp), w_rows(dp), wx_s.at[d - 1], wx_r.at[d - 1], (lax.rem(x + d, NX) * NC + core, e)).start()
    remote(w_rows(dp), w_rows(dp), wc_s.at[0], wc_r.at[0], pair).start()
    for d in range(1, NY):
        yy = lax.rem(y + d, NY)
        remote(tok_cols(yy), tokg.at[dp, y], t1_s, t1_r, (dp, yy * NZ + z)).start()
    pltpu.make_async_copy(tok_cols(y), tokg.at[dp, y], t1_r).start()

    mine = dp * NY + y

    def spread_early(i, c):
        to_dp, to_y = lax.rem(dp + i // NY, NDP), lax.rem(y + i, NY)
        remote(esend.at[to_dp], erecv.at[mine], e_s, e_r, (to_dp, to_y * NZ + z)).start()
        return c

    lax.fori_loop(1, NDP * NY, spread_early, 0)
    pltpu.make_async_copy(esend.at[dp], erecv.at[mine], e_r).start()

    pos, gate = slots(own_meta[...])
    posv[...] = pos
    dispatch(0, og[:, :H], og[:, H:], pos, gate)
    load.wait()
    savedf[...] = savedv[...].astype(F32).reshape(NY, NZ, 8, FW)

    for st in range(1, RE):
        for c in range(2):
            for g in range(2):
                arrived(g, st - 1, c)
                hop(g, st, c)
        for g in range(2):
            pos, gate = slots(meta[g * RE + st - 1])
            dispatch(2 * st - 1 + g, ring[g, st - 1, 0], ring[g, st - 1, 1], pos, gate)
        if st == max(RE - 2, 1):
            for d in range(1, NX):
                shard = lax.rem(x + NX - d, NX) * NC + core
                drain(w_rows(shard), wx_r.at[d - 1])
                remote(w_rows(shard), w_rows(shard), wc_s.at[d], wc_r.at[d], pair).start()
            drain(tokg.at[dp], t1_r)
            for d in range(1, NX):
                to = (lax.rem(x + d, NX) * NC + core, e)
                remote(tokg.at[dp], tokg.at[dp], tx_s.at[d - 1], tx_r.at[d - 1], to).start()
            remote(tokg.at[dp], tokg.at[dp], tc_s.at[0], tc_r.at[0], pair).start()

    def joined(block, n, width):
        v = block.astype(F32)
        low = v[:, :8].reshape(n * 8, width)
        high = v[:, 8:].reshape(n * 8, width)
        return jnp.concatenate([low, high], axis=1).astype(BF16)

    def finish(f, g, backs, columns, sources):
        for i, zs in enumerate(sources):
            part = g[i * NY * 8 : (i + 1) * NY * 8].reshape(NY, 8, FC)
            hidf[:, zs, :, f : f + FC] = columns[i] * part
            backs[i] = backs[i] + jnp.sum(savedf[:, zs, :, f : f + FC] * part, axis=2, keepdims=True)

    def column(rows):
        return jnp.sum(jnp.where(lane8, rows, 0.0), axis=2, keepdims=True)

    def give_back(i, zs, back):
        rsend[i] = jnp.sum(jnp.where(lane8, back, 0.0), axis=1, keepdims=True)
        for d in range(NY):
            yy = lax.rem(y + d, NY)
            if i == 0 and d == 0:
                pltpu.make_async_copy(rsend.at[i, yy], rrecv.at[e], ret_r).start()
            else:
                remote(rsend.at[i, yy], rrecv.at[e], ret_s, ret_r, (dp, yy * NZ + zs)).start()

    def near(group):
        sources = []
        for ni in group:
            drain(nrecv.at[ni], near_r.at[ni])
            drain(gnrecv.at[ni], gn_r.at[ni])
            st = (ni + 1) // 2
            sources.append(lax.rem(z + (NZ - st if ni % 2 == 1 else st), NZ))
        rows = jnp.concatenate([joined(nrecv[ni], NY, H) for ni in group], axis=0)
        columns = [column(gnrecv[ni]) for ni in group]
        backs = [jnp.zeros((NY, 8, 1), F32) for ni in group]
        for f in range(0, FW, FC):
            g = lax.dot_general(rows, wfull[f : f + FC], nt, preferred_element_type=F32)
            finish(f, g, backs, columns, sources)
        for ni, zs, back in zip(group, sources, backs):
            give_back(ni, zs, back)

    for c in range(2):
        for g in range(2):
            arrived(g, RE - 1, c)
            relay(g, c)
    for g in range(2):
        pos, gate = slots(meta[g * RE + RE - 1])
        dispatch(2 * RE - 1 + g, ring[g, RE - 1, 0], ring[g, RE - 1, 1], pos, gate)
    for d in range(NX):
        shard = lax.rem(x + NX - d, NX) * NC + 1 - core
        drain(w_rows(shard), wc_r.at[d])
    near([0, 1, 2])
    for first in range(3, NN, 4):
        near(list(range(first, min(first + 4, NN))))
    for d in range(1, NX):
        shard = lax.rem(x + NX - d, NX) * NC + core
        drain(tokg.at[shard], tx_r.at[d - 1])
        remote(tokg.at[shard], tokg.at[shard], tc_s.at[d], tc_r.at[d], pair).start()

    drain(frecv.at[0], far_r.at[0])
    rows = joined(frecv[0].reshape(NF * NY, 16, H // 2), NF * NY, H // 2)
    for f in range(0, FW, FC):
        half[:, f : f + FC] = lax.dot_general(rows, wfull[f : f + FC, :H], nt, preferred_element_type=F32)
    drain(gfrecv, gf_r)
    columns = [column(gfrecv[i]) for i in range(NF)]
    backs = [jnp.zeros((NY, 8, 1), F32) for i in range(NF)]
    sources = [lax.rem(z + (NZ - RE - 1 - i if i < RE else i + 1), NZ) for i in range(NF)]
    drain(frecv.at[1], far_r.at[1])
    rows = joined(frecv[1].reshape(NF * NY, 16, H // 2), NF * NY, H // 2)
    for f in range(0, FW, FC):
        g = lax.dot_general(rows, wfull[f : f + FC, H:], nt, preferred_element_type=F32)
        finish(f, g + half[:, f : f + FC], backs, columns, sources)
    for i in range(NF):
        give_back(NN + i, sources[i], backs[i])
    hid[...] = hidf[...].reshape(NY, NZ * 8, FW).astype(BF16)
    for d in range(NX):
        shard = lax.rem(x + NX - d, NX) * NC + 1 - core
        drain(tokg.at[shard], tc_r.at[d])

    drain(rrecv, ret_r)
    ret = rrecv[...].reshape(NE, 128)
    pos = posv[...]
    grad_e = jnp.zeros((NE, T), F32)
    for c in range(8):
        grad_e = jnp.where(pos == float(c), ret[:, c : c + 1], grad_e)
    scores, gates, ssum = small[0], small[1], small[2]
    k_rows = [ids[k : k + 1, :] for k in range(8)]
    window = iota((NE, T), 0)
    choice = jnp.concatenate(
        [jnp.sum(jnp.where(window == row, grad_e, 0.0), axis=0, keepdims=True) for row in k_rows], axis=0
    )
    mixed = jnp.sum(choice * gates, axis=0, keepdims=True) / RSCALE
    dchosen = RSCALE / ssum * (choice - mixed) * scores * (1.0 - scores)
    dsend[...] = dchosen

    def spread_d(i, c):
        to_dp, to_y = lax.rem(dp + i // NY, NDP), lax.rem(y + i, NY)
        remote(dsend, drecv.at[mine], d_s, d_r.at[dp], (to_dp, to_y * NZ + z)).start()
        return c

    lax.fori_loop(1, NDP * NY, spread_d, 0)
    pltpu.make_async_copy(dsend, drecv.at[mine], d_r.at[dp]).start()
    names = iota((EX, T), 0)
    lgt = zterm[...]
    for k, row in enumerate(k_rows):
        lgt = lgt + jnp.where(names == row, dchosen[k : k + 1, :], 0.0)
    lg[...] = lgt.reshape(NDP, ED, T)

    drain(erecv, e_r)
    own_names = (iota((ED, T), 0) + dp * ED).astype(F32)
    panel = jnp.zeros((2 * ED, Q), F32)
    for i in range(NDP):
        owner = lax.rem(dp + i, NDP)
        drain(drecv.at[pl.ds(owner * NY, NY)], d_r.at[owner])
        parts = []
        for yy in range(NY):
            at = owner * NY + yy
            early, late = erecv[at], drecv[at]
            v = early[:ED]
            for k in range(8):
                v = v + jnp.where(early[ED + k : ED + k + 1] == own_names, late[k : k + 1], 0.0)
            parts.append(v)
        v = jnp.concatenate(parts, axis=1)
        hi = v.astype(BF16).astype(F32)
        both = jnp.concatenate([v, v - hi], axis=0).astype(BF16)
        panel = panel + jnp.dot(both, tokg[owner].reshape(NY * T, Q), preferred_element_type=F32)
    panel = panel[:ED] + panel[ED:]
    blank = jnp.zeros((16, 64 - R), F32) if R < 64 else None
    for j in range(NZ):
        piece = panel[:, j * R : (j + 1) * R]
        sides = [piece[:16], jnp.concatenate([piece[16:], jnp.zeros((32 - ED, R), F32)], axis=0)]
        if R < 64:
            sides = [sides[0], blank, sides[1], blank]
        zsend[j] = jnp.concatenate(sides, axis=1).astype(BF16)

    def spread_z(i, c):
        to = lax.rem(z + i, NZ)
        remote(zsend.at[to], zrecv.at[z], z_s, z_r, (dp, y * NZ + to)).start()
        return c

    lax.fori_loop(1, NZ, spread_z, 0)
    pltpu.make_async_copy(zsend.at[z], zrecv.at[z], z_r).start()
    drain(zrecv, z_r)
    out = jnp.sum(zrecv[...].astype(F32), axis=0)
    rg[:16] = out[:, :R]
    rg[16:] = out[: ED - 16, 64 : 64 + R]

    for g in range(2):
        for st in range(RE):
            drain(meta.at[0], meta_s.at[g, st])
            for c in range(2):
                drain(ring.at[0, 0, 0], ring_s.at[g, st, c])
    drain(nsend.at[:, pl.ds(0, NY - 1)], near_s)
    drain(gnsend.at[:, pl.ds(0, NY - 1)], gn_s)
    drain(frecv, far_s)
    drain(gfrecv, gf_s)
    drain(rsend.at[pl.ds(1, NZ - 1)], ret_s)
    drain(rsend.at[0, pl.ds(0, NY - 1)], ret_s)
    for d in range(NX - 1):
        drain(w_rows(dp), wx_s.at[d])
        drain(tokg.at[dp], tx_s.at[d])
    for d in range(NX):
        drain(w_rows(dp), wc_s.at[d])
        drain(tokg.at[dp], tc_s.at[d])
    drain(tokg.at[dp, pl.ds(0, NY - 1)], t1_s)
    drain(erecv.at[pl.ds(0, NDP * NY - 1)], e_s)
    drain(drecv.at[pl.ds(0, NDP * NY - 1)], d_s)
    drain(zsend.at[pl.ds(0, NZ - 1)], z_s)


def local(dims, tokens_in, out_grad, router_logits, expert_ids, saved_hidden, down_weight):
    NX, NY, NZ = dims
    NDP, NE = NX * NC, NY * NZ
    RE = NZ // 4
    NN, NF = 2 * RE + 1, 2 * RE - 1
    T, D = out_grad.shape
    H = D // 2
    FW = saved_hidden.shape[4]
    EX = router_logits.shape[1]
    ED, Q, R = EX // NDP, D // NY, D // NE
    vmem = pl.BlockSpec(memory_space=pltpu.VMEM)
    hbm = pl.BlockSpec(memory_space=pl.ANY)
    dma = pltpu.SemaphoreType.DMA
    one = dma(())
    hid, lg, rg = pl.pallas_call(
        functools.partial(kernel, dims),
        out_shape=(
            pltpu.VMEM((NY, NZ * 8, FW), BF16),
            pltpu.VMEM((NDP, ED, T), F32),
            pltpu.VMEM((ED, R), F32),
        ),
        in_specs=[hbm] * 6,
        out_specs=(vmem, vmem, vmem),
        scratch_shapes=[
            pltpu.VMEM((2, RE, 2, T, H), BF16),
            pltpu.VMEM((2 * RE + 1, 16, T), BF16),
            pltpu.VMEM((NN, NY, 16, H), BF16),
            pltpu.VMEM((NN, NY, 16, H), BF16),
            pltpu.VMEM((2, 2, RE * NY, 16, H // 2), BF16),
            pltpu.VMEM((2, NF, NY, 16, H // 2), BF16),
            pltpu.VMEM((2, RE * NY * 8, T), BF16),
            pltpu.VMEM((NN, NY, 1, 128), F32),
            pltpu.VMEM((NN, NY, 1, 128), F32),
            pltpu.VMEM((2, RE * NY, 1, 128), F32),
            pltpu.VMEM((NF, NY, 1, 128), F32),
            pltpu.VMEM((NF * NY * 8, FW), F32),
            pltpu.VMEM((FW, D), BF16),
            pltpu.VMEM((NDP, NY, T, Q), BF16),
            pltpu.VMEM((NY, NZ * 8, FW), BF16),
            pltpu.VMEM((NY, NZ, 8, FW), F32),
            pltpu.VMEM((NY, NZ, 8, FW), F32),
            pltpu.VMEM((NZ, NY, 1, 128), F32),
            pltpu.VMEM((NE, 1, 128), F32),
            pltpu.VMEM((NDP, ED + 8, T), F32),
            pltpu.VMEM((NDP * NY, ED + 8, T), F32),
            pltpu.VMEM((8, T), F32),
            pltpu.VMEM((NDP * NY, 8, T), F32),
            pltpu.VMEM((NZ, 16, 128), BF16),
            pltpu.VMEM((NZ, 16, 128), BF16),
            pltpu.VMEM((EX, T), F32),
            pltpu.VMEM((NE, T), F32),
            pltpu.VMEM((3, 8, T), F32),
            pltpu.VMEM((T, D), BF16),
            pltpu.VMEM((EX, T), F32),
            pltpu.VMEM((8, T), jnp.int32),
            dma((2, RE, 2)), dma((2, RE, 2)), dma((2, RE)), dma((2, RE)),
            one, dma((NN,)), one, dma((NN,)), one, dma((2,)), one, one, one, one,
            dma((NX - 1,)), dma((NX - 1,)), dma((NX,)), dma((NX,)),
            one, one, dma((NX - 1,)), dma((NX - 1,)), dma((NX,)), dma((NX,)),
            one, one, one, dma((NDP,)), one, one, dma((5,)),
        ],
        compiler_params=pltpu.CompilerParams(
            collective_id=0, has_side_effects=True, vmem_limit_bytes=58 * 2**20
        ),
        cost_estimate=pl.CostEstimate(flops=4 * 10**9, bytes_accessed=6 * 10**6, transcendentals=0),
    )(
        out_grad,
        router_logits.T,
        expert_ids.T,
        tokens_in,
        down_weight.reshape(FW // NDP, D),
        saved_hidden.reshape(NY, NZ * 8, FW),
    )
    return hid.reshape(1, 1, NE, 8, FW), lg.reshape(EX, T).T, rg.T


def solution(mesh, dims=(4, 4, 16)):
    in_specs = (
        P(("dp", "expert"), None),
        P(("dp", "expert"), None),
        P(("dp", "expert"), None),
        P(("dp", "expert"), None),
        P("dp", "expert", None, None, None),
        P("expert", "dp", None),
    )
    out_specs = (P("dp", "expert", None, None, None), P(("dp", "expert"), None), P("expert", "dp"))
    return jax.shard_map(
        functools.partial(local, dims), mesh=mesh, in_specs=in_specs, out_specs=out_specs, check_vma=False
    )
```

```python
import functools

import jax
import jax.numpy as jnp
from jax import lax
from jax.experimental import pallas as pl
from jax.experimental.pallas import tpu as pltpu
from jax.sharding import PartitionSpec as P

RSCALE = 2.827
ZLOSS = 0.25
NC = 2
MESH = pl.DeviceIdType.MESH
F32 = jnp.float32
BF16 = jnp.bfloat16


def drain(ref, sem):
    pltpu.make_async_copy(ref, ref, sem).wait()


def iota(shape, dim):
    return lax.broadcasted_iota(jnp.int32, shape, dim)


def kernel(
    dims,
    og_in, logits_in, ids_in, tok, w, saved,
    hid, lg, rg,
    ring, meta, nsend, nrecv, fsend, frecv, ftable, gnsend, gnrecv, gfsend, gfrecv, half,
    wfull, tokg, savedv, savedf, hidf, rsend, rrecv, esend, erecv, dsend, drecv, zsend, zrecv, zterm, posv, small, og, logits, ids,
    ring_s, ring_r, meta_s, meta_r, near_s, near_r, gn_s, gn_r, far_s, far_r, gf_s, gf_r, ret_s, ret_r,
    wx_s, wx_r, wc_s, wc_r, t1_s, t1_r, tx_s, tx_r, tc_s, tc_r, e_s, e_r, d_s, d_r, z_s, z_r, local_sem,
):
    NX, NY, NZ = dims
    NDP, NE = NX * NC, NY * NZ
    RE = NZ // 4
    NN, NF = 2 * RE + 1, 2 * RE - 1
    T, D = og_in.shape
    H = D // 2
    Q = D // NY
    FW = wfull.shape[0]
    FS = FW // NDP
    FC = min(FW, 256)
    EX = logits_in.shape[0]
    ED = EX // NDP
    R = D // NE
    dp, e = lax.axis_index("dp"), lax.axis_index("expert")
    x, core = dp // NC, dp % NC
    y, z = e // NZ, e % NZ
    nt = (((1,), (1,)), ((), ()))

    def remote(src, dst, s, r, dev):
        return pltpu.make_async_remote_copy(
            src_ref=src, dst_ref=dst, send_sem=s, recv_sem=r, device_id=dev, device_id_type=MESH
        )

    loads = [
        pltpu.make_async_copy(src, dst, local_sem.at[2 + i])
        for i, (src, dst) in enumerate(((logits_in, logits), (ids_in, ids), (og_in, og)))
    ]
    for copy in loads:
        copy.start()

    barrier = pltpu.get_barrier_semaphore()

    def greet(i, c):
        away = jnp.where(i % 2 == 1, (i + 1) // 2, NE - i // 2)
        pl.semaphore_signal(barrier, inc=1, device_id=(dp, lax.rem(e + away, NE)), device_id_type=MESH)
        return c

    lax.fori_loop(1, NE, greet, 0)

    def greet2(i, c):
        other = lax.rem(dp + 1 + i // NY, NDP)
        pl.semaphore_signal(barrier, inc=1, device_id=(other, lax.rem(i, NY) * NZ + z), device_id_type=MESH)
        return c

    lax.fori_loop(0, (NDP - 1) * NY, greet2, 0)
    load = pltpu.make_async_copy(saved, savedv, local_sem.at[0])
    load.start()
    own_w = pltpu.make_async_copy(w, wfull.at[pl.ds(pl.multiple_of(dp * FS, FS), FS)], local_sem.at[1])
    own_w.start()

    lane8 = iota((NY, 8, 128), 2) == iota((NY, 8, 128), 1)

    def slots(info):
        info = info.astype(F32)
        window = iota((NE, T), 0).astype(F32)
        mask = jnp.zeros((NE, T), F32)
        gate = jnp.zeros((NE, T), F32)
        for k in range(8):
            hit = window == info[k : k + 1, :]
            mask = jnp.where(hit, 1.0, mask)
            gate = jnp.where(hit, info[8 + k : 9 + k, :], gate)
        earlier = (iota((T, T), 0) < iota((T, T), 1)).astype(F32).astype(BF16)
        rank = jnp.dot(mask.astype(BF16), earlier, preferred_element_type=F32)
        return jnp.where(mask > 0.0, rank, 255.0), gate

    def tables(pos, gate, experts):
        n = experts.shape[0]
        pick = (iota((n, NE), 1) == experts).astype(F32).astype(BF16)
        spread = jnp.dot(pick, pos.astype(BF16), preferred_element_type=F32)
        hit = spread == (iota((n, T), 0) % 8).astype(F32)
        gates_at = jnp.dot(pick, gate.astype(BF16), preferred_element_type=F32)
        col = jnp.sum(jnp.where(hit, gates_at, 0.0), axis=1, keepdims=True).reshape(n // 8, 8, 1)
        at = iota((n // 8, 8, 128), 2) == iota((n // 8, 8, 128), 1)
        return hit.astype(F32).astype(BF16), jnp.sum(jnp.where(at, col, 0.0), axis=1, keepdims=True)

    def dispatch(ni, low, high, pos, gate):
        experts = iota((NY * 8, 1), 0) // 8 * NZ + z
        table, rows = tables(pos, gate, experts)
        gnsend[ni] = rows
        a = jnp.dot(table, low, preferred_element_type=F32).reshape(NY, 8, H)
        b = jnp.dot(table, high, preferred_element_type=F32).reshape(NY, 8, H)
        nsend[ni] = jnp.concatenate([a, b], axis=1).astype(BF16)
        for d in range(1, NY):
            yy = lax.rem(y + d, NY)
            remote(nsend.at[ni, yy], nrecv.at[ni, y], near_s, near_r.at[ni], (dp, yy * NZ + z)).start()
            remote(gnsend.at[ni, yy], gnrecv.at[ni, y], gn_s, gn_r.at[ni], (dp, yy * NZ + z)).start()
        pltpu.make_async_copy(nsend.at[ni, y], nrecv.at[ni, y], near_r.at[ni]).start()
        pltpu.make_async_copy(gnsend.at[ni, y], gnrecv.at[ni, y], gn_r.at[ni]).start()

    def hop_meta(g, st):
        to = (dp, y * NZ + lax.rem(z + (1 if g == 0 else NZ - 1), NZ))
        info = meta.at[2 * RE] if st == 0 else meta.at[g * RE + st - 1]
        remote(info, meta.at[g * RE + st], meta_s.at[g, st], meta_r.at[g, st], to).start()

    def hop(g, st, c):
        to = (dp, y * NZ + lax.rem(z + (1 if g == 0 else NZ - 1), NZ))
        src = og_in.at[:, pl.ds(c * H, H)] if st == 0 else ring.at[g, st - 1, c]
        remote(src, ring.at[g, st, c], ring_s.at[g, st, c], ring_r.at[g, st, c], to).start()
        if c == 0 and st > 0:
            hop_meta(g, st)

    def arrived(g, st, c):
        if c == 0:
            drain(meta.at[g * RE + st], meta_r.at[g, st])
        drain(ring.at[g, st, c], ring_r.at[g, st, c])

    def relay(g, c):
        n = RE * NY
        if c == 0:
            d = iota((n * 8, 1), 0) // 8
            step = d // NY + 1
            experts = (y + d % NY) % NY * NZ + (z + (step if g == 0 else NZ - step)) % NZ
            pos, gate = slots(meta[g * RE + RE - 1])
            table, rows = tables(pos, gate, experts)
            ftable[g] = table
            gfsend[g] = rows
        p = jnp.dot(ftable[g], ring[g, RE - 1, c], preferred_element_type=F32).reshape(n, 8, H)
        fsend[c, g] = jnp.concatenate([p[:, :, : H // 2], p[:, :, H // 2 :]], axis=1).astype(BF16)

        def one(d, carry):
            j = d // NY + 1
            to = (dp, lax.rem(y + d % NY, NY) * NZ + lax.rem(z + (j if g == 0 else NZ - j), NZ))
            fi = j - 1 if g == 0 else jnp.where(j == RE, RE - 1, RE - 1 + j)
            remote(fsend.at[c, g, d], frecv.at[c, fi, y], far_s, far_r.at[c], to).start()
            if c == 0:
                remote(gfsend.at[g, d], gfrecv.at[fi, y], gf_s, gf_r, to).start()
            return carry

        last = (RE - 1) * NY
        split = last + NY // 2
        lax.fori_loop(*((last, split) if g == 0 else (split, RE * NY)), one, 0)
        lax.fori_loop(0, last, lambda i, carry: one(last - 1 - i, carry), 0)

    def w_rows(owner):
        return wfull.at[pl.ds(pl.multiple_of(owner * FS, FS), FS)]

    def tok_cols(yy):
        return tok.at[:, pl.ds(pl.multiple_of(yy * Q, 128), Q)]

    pair = (x * NC + 1 - core, e)
    pl.semaphore_wait(barrier, NE - 1 + (NDP - 1) * NY)

    for c in range(2):
        for g in range(2):
            hop(g, 0, c)
    for d in range(1, NX):
        remote(w, w_rows(dp), wx_s.at[d - 1], wx_r.at[d - 1], (lax.rem(x + d, NX) * NC + core, e)).start()
    remote(w, w_rows(dp), wc_s.at[0], wc_r.at[0], pair).start()
    for d in range(1, NY):
        yy = lax.rem(y + d, NY)
        remote(tok_cols(yy), tokg.at[dp, y], t1_s, t1_r, (dp, yy * NZ + z)).start()
    pltpu.make_async_copy(tok_cols(y), tokg.at[dp, y], t1_r).start()

    loads[0].wait()
    loads[1].wait()
    lt = logits[...]
    top = jnp.max(lt, axis=0, keepdims=True)
    shifted = jnp.exp(lt - top)
    total = jnp.sum(shifted, axis=0, keepdims=True)
    lse = top + jnp.log(total)
    zterm[...] = (2.0 * ZLOSS) * lse * (shifted / total)
    names = iota((EX, T), 0)
    k_rows = [ids[k : k + 1, :] for k in range(8)]
    chosen = jnp.concatenate(
        [jnp.sum(jnp.where(names == row, lt, 0.0), axis=0, keepdims=True) for row in k_rows], axis=0
    )
    scores = 1.0 / (1.0 + jnp.exp(-chosen))
    ssum = jnp.sum(scores, axis=0, keepdims=True)
    gates = RSCALE * scores / ssum
    small[0] = scores
    small[1] = gates
    small[2] = jnp.broadcast_to(ssum, scores.shape)
    own_meta = meta.at[2 * RE]
    names_f = ids[...].astype(F32)
    own_meta[...] = jnp.concatenate([names_f, gates], axis=0).astype(BF16)
    for d in range(NDP):
        esend[d, :ED] = zterm[d * ED : (d + 1) * ED]
        esend[d, ED:] = names_f
    loads[2].wait()
    for g in range(2):
        hop_meta(g, 0)
    mine = dp * NY + y

    def spread_early(i, c):
        to_dp, to_y = lax.rem(dp + i // NY, NDP), lax.rem(y + i, NY)
        remote(esend.at[to_dp], erecv.at[mine], e_s, e_r, (to_dp, to_y * NZ + z)).start()
        return c

    lax.fori_loop(1, NDP * NY, spread_early, 0)
    pltpu.make_async_copy(esend.at[dp], erecv.at[mine], e_r).start()

    pos, gate = slots(own_meta[...])
    posv[...] = pos
    dispatch(0, og[:, :H], og[:, H:], pos, gate)
    load.wait()
    savedf[...] = savedv[...].astype(F32).reshape(NY, NZ, 8, FW)

    for st in range(1, RE):
        for c in range(2):
            for g in range(2):
                arrived(g, st - 1, c)
                hop(g, st, c)
        for g in range(2):
            pos, gate = slots(meta[g * RE + st - 1])
            dispatch(2 * st - 1 + g, ring[g, st - 1, 0], ring[g, st - 1, 1], pos, gate)
        if st == max(RE - 2, 1):
            for d in range(1, NX):
                shard = lax.rem(x + NX - d, NX) * NC + core
                drain(w_rows(shard), wx_r.at[d - 1])
                remote(w_rows(shard), w_rows(shard), wc_s.at[d], wc_r.at[d], pair).start()
            drain(tokg.at[dp], t1_r)
            for d in range(1, NX):
                to = (lax.rem(x + d, NX) * NC + core, e)
                remote(tokg.at[dp], tokg.at[dp], tx_s.at[d - 1], tx_r.at[d - 1], to).start()
            remote(tokg.at[dp], tokg.at[dp], tc_s.at[0], tc_r.at[0], pair).start()

    def joined(block, n, width):
        v = block.astype(F32)
        low = v[:, :8].reshape(n * 8, width)
        high = v[:, 8:].reshape(n * 8, width)
        return jnp.concatenate([low, high], axis=1).astype(BF16)

    def finish(f, g, backs, columns, sources):
        for i, zs in enumerate(sources):
            part = g[i * NY * 8 : (i + 1) * NY * 8].reshape(NY, 8, FC)
            hidf[:, zs, :, f : f + FC] = columns[i] * part
            backs[i] = backs[i] + jnp.sum(savedf[:, zs, :, f : f + FC] * part, axis=2, keepdims=True)

    def column(rows):
        return jnp.sum(jnp.where(lane8, rows, 0.0), axis=2, keepdims=True)

    def give_back(i, zs, back):
        rsend[i] = jnp.sum(jnp.where(lane8, back, 0.0), axis=1, keepdims=True)
        for d in range(NY):
            yy = lax.rem(y + d, NY)
            if i == 0 and d == 0:
                pltpu.make_async_copy(rsend.at[i, yy], rrecv.at[e], ret_r).start()
            else:
                remote(rsend.at[i, yy], rrecv.at[e], ret_s, ret_r, (dp, yy * NZ + zs)).start()

    def near(group):
        sources = []
        for ni in group:
            drain(nrecv.at[ni], near_r.at[ni])
            drain(gnrecv.at[ni], gn_r.at[ni])
            st = (ni + 1) // 2
            sources.append(lax.rem(z + (NZ - st if ni % 2 == 1 else st), NZ))
        rows = jnp.concatenate([joined(nrecv[ni], NY, H) for ni in group], axis=0)
        columns = [column(gnrecv[ni]) for ni in group]
        backs = [jnp.zeros((NY, 8, 1), F32) for ni in group]
        for f in range(0, FW, FC):
            g = lax.dot_general(rows, wfull[f : f + FC], nt, preferred_element_type=F32)
            finish(f, g, backs, columns, sources)
        for ni, zs, back in zip(group, sources, backs):
            give_back(ni, zs, back)

    for c in range(2):
        for g in range(2):
            arrived(g, RE - 1, c)
            relay(g, c)
    for g in range(2):
        pos, gate = slots(meta[g * RE + RE - 1])
        dispatch(2 * RE - 1 + g, ring[g, RE - 1, 0], ring[g, RE - 1, 1], pos, gate)
    for d in range(NX):
        shard = lax.rem(x + NX - d, NX) * NC + 1 - core
        drain(w_rows(shard), wc_r.at[d])
    own_w.wait()
    near([0, 1, 2])
    for first in range(3, NN, 4):
        near(list(range(first, min(first + 4, NN))))
    for d in range(1, NX):
        shard = lax.rem(x + NX - d, NX) * NC + core
        drain(tokg.at[shard], tx_r.at[d - 1])
        remote(tokg.at[shard], tokg.at[shard], tc_s.at[d], tc_r.at[d], pair).start()

    drain(frecv.at[0], far_r.at[0])
    rows = joined(frecv[0].reshape(NF * NY, 16, H // 2), NF * NY, H // 2)
    for f in range(0, FW, FC):
        half[:, f : f + FC] = lax.dot_general(rows, wfull[f : f + FC, :H], nt, preferred_element_type=F32)
    drain(gfrecv, gf_r)
    columns = [column(gfrecv[i]) for i in range(NF)]
    backs = [jnp.zeros((NY, 8, 1), F32) for i in range(NF)]
    sources = [lax.rem(z + (NZ - RE - 1 - i if i < RE else i + 1), NZ) for i in range(NF)]
    drain(frecv.at[1], far_r.at[1])
    rows = joined(frecv[1].reshape(NF * NY, 16, H // 2), NF * NY, H // 2)
    for f in range(0, FW, FC):
        g = lax.dot_general(rows, wfull[f : f + FC, H:], nt, preferred_element_type=F32)
        finish(f, g + half[:, f : f + FC], backs, columns, sources)
    for i in range(NF):
        give_back(NN + i, sources[i], backs[i])
    hid[...] = hidf[...].reshape(NY, NZ * 8, FW).astype(BF16)
    for d in range(NX):
        shard = lax.rem(x + NX - d, NX) * NC + 1 - core
        drain(tokg.at[shard], tc_r.at[d])

    drain(rrecv, ret_r)
    ret = rrecv[...].reshape(NE, 128)
    pos = posv[...]
    grad_e = jnp.zeros((NE, T), F32)
    for c in range(8):
        grad_e = jnp.where(pos == float(c), ret[:, c : c + 1], grad_e)
    scores, gates, ssum = small[0], small[1], small[2]
    k_rows = [ids[k : k + 1, :] for k in range(8)]
    window = iota((NE, T), 0)
    choice = jnp.concatenate(
        [jnp.sum(jnp.where(window == row, grad_e, 0.0), axis=0, keepdims=True) for row in k_rows], axis=0
    )
    mixed = jnp.sum(choice * gates, axis=0, keepdims=True) / RSCALE
    dchosen = RSCALE / ssum * (choice - mixed) * scores * (1.0 - scores)
    dsend[...] = dchosen

    def spread_d(i, c):
        to_dp, to_y = lax.rem(dp + i // NY, NDP), lax.rem(y + i, NY)
        remote(dsend, drecv.at[mine], d_s, d_r.at[dp], (to_dp, to_y * NZ + z)).start()
        return c

    lax.fori_loop(1, NDP * NY, spread_d, 0)
    pltpu.make_async_copy(dsend, drecv.at[mine], d_r.at[dp]).start()
    names = iota((EX, T), 0)
    lgt = zterm[...]
    for k, row in enumerate(k_rows):
        lgt = lgt + jnp.where(names == row, dchosen[k : k + 1, :], 0.0)
    lg[...] = lgt.reshape(NDP, ED, T)

    drain(erecv, e_r)
    own_names = (iota((ED, T), 0) + dp * ED).astype(F32)
    panel = jnp.zeros((2 * ED, Q), F32)
    for i in range(NDP):
        owner = lax.rem(dp + NDP - i, NDP)
        drain(drecv.at[pl.ds(owner * NY, NY)], d_r.at[owner])
        parts = []
        for yy in range(NY):
            at = owner * NY + yy
            early, late = erecv[at], drecv[at]
            v = early[:ED]
            for k in range(8):
                v = v + jnp.where(early[ED + k : ED + k + 1] == own_names, late[k : k + 1], 0.0)
            parts.append(v)
        v = jnp.concatenate(parts, axis=1)
        hi = v.astype(BF16).astype(F32)
        both = jnp.concatenate([v, v - hi], axis=0).astype(BF16)
        panel = panel + jnp.dot(both, tokg[owner].reshape(NY * T, Q), preferred_element_type=F32)
    panel = panel[:ED] + panel[ED:]
    blank = jnp.zeros((16, 64 - R), F32) if R < 64 else None
    for j in range(NZ):
        piece = panel[:, j * R : (j + 1) * R]
        sides = [piece[:16], jnp.concatenate([piece[16:], jnp.zeros((32 - ED, R), F32)], axis=0)]
        if R < 64:
            sides = [sides[0], blank, sides[1], blank]
        zsend[j] = jnp.concatenate(sides, axis=1).astype(BF16)

    def spread_z(i, c):
        to = lax.rem(z + i, NZ)
        remote(zsend.at[to], zrecv.at[z], z_s, z_r, (dp, y * NZ + to)).start()
        return c

    lax.fori_loop(1, NZ, spread_z, 0)
    pltpu.make_async_copy(zsend.at[z], zrecv.at[z], z_r).start()
    drain(zrecv, z_r)
    out = jnp.sum(zrecv[...].astype(F32), axis=0)
    rg[:16] = out[:, :R]
    rg[16:] = out[: ED - 16, 64 : 64 + R]

    for g in range(2):
        for st in range(RE):
            drain(meta.at[0], meta_s.at[g, st])
            for c in range(2):
                drain(ring.at[0, 0, 0], ring_s.at[g, st, c])
    drain(nsend.at[:, pl.ds(0, NY - 1)], near_s)
    drain(gnsend.at[:, pl.ds(0, NY - 1)], gn_s)
    drain(frecv, far_s)
    drain(gfrecv, gf_s)
    drain(rsend.at[pl.ds(1, NZ - 1)], ret_s)
    drain(rsend.at[0, pl.ds(0, NY - 1)], ret_s)
    for d in range(NX - 1):
        drain(w_rows(dp), wx_s.at[d])
        drain(tokg.at[dp], tx_s.at[d])
    for d in range(NX):
        drain(w_rows(dp), wc_s.at[d])
        drain(tokg.at[dp], tc_s.at[d])
    drain(tokg.at[dp, pl.ds(0, NY - 1)], t1_s)
    drain(erecv.at[pl.ds(0, NDP * NY - 1)], e_s)
    drain(drecv.at[pl.ds(0, NDP * NY - 1)], d_s)
    drain(zsend.at[pl.ds(0, NZ - 1)], z_s)


def local(dims, tokens_in, out_grad, router_logits, expert_ids, saved_hidden, down_weight):
    NX, NY, NZ = dims
    NDP, NE = NX * NC, NY * NZ
    RE = NZ // 4
    NN, NF = 2 * RE + 1, 2 * RE - 1
    T, D = out_grad.shape
    H = D // 2
    FW = saved_hidden.shape[4]
    EX = router_logits.shape[1]
    ED, Q, R = EX // NDP, D // NY, D // NE
    vmem = pl.BlockSpec(memory_space=pltpu.VMEM)
    hbm = pl.BlockSpec(memory_space=pl.ANY)
    dma = pltpu.SemaphoreType.DMA
    one = dma(())
    hid, lg, rg = pl.pallas_call(
        functools.partial(kernel, dims),
        out_shape=(
            pltpu.VMEM((NY, NZ * 8, FW), BF16),
            pltpu.VMEM((NDP, ED, T), F32),
            pltpu.VMEM((ED, R), F32),
        ),
        in_specs=[hbm] * 6,
        out_specs=(vmem, vmem, vmem),
        scratch_shapes=[
            pltpu.VMEM((2, RE, 2, T, H), BF16),
            pltpu.VMEM((2 * RE + 1, 16, T), BF16),
            pltpu.VMEM((NN, NY, 16, H), BF16),
            pltpu.VMEM((NN, NY, 16, H), BF16),
            pltpu.VMEM((2, 2, RE * NY, 16, H // 2), BF16),
            pltpu.VMEM((2, NF, NY, 16, H // 2), BF16),
            pltpu.VMEM((2, RE * NY * 8, T), BF16),
            pltpu.VMEM((NN, NY, 1, 128), F32),
            pltpu.VMEM((NN, NY, 1, 128), F32),
            pltpu.VMEM((2, RE * NY, 1, 128), F32),
            pltpu.VMEM((NF, NY, 1, 128), F32),
            pltpu.VMEM((NF * NY * 8, FW), F32),
            pltpu.VMEM((FW, D), BF16),
            pltpu.VMEM((NDP, NY, T, Q), BF16),
            pltpu.VMEM((NY, NZ * 8, FW), BF16),
            pltpu.VMEM((NY, NZ, 8, FW), F32),
            pltpu.VMEM((NY, NZ, 8, FW), F32),
            pltpu.VMEM((NZ, NY, 1, 128), F32),
            pltpu.VMEM((NE, 1, 128), F32),
            pltpu.VMEM((NDP, ED + 8, T), F32),
            pltpu.VMEM((NDP * NY, ED + 8, T), F32),
            pltpu.VMEM((8, T), F32),
            pltpu.VMEM((NDP * NY, 8, T), F32),
            pltpu.VMEM((NZ, 16, 128), BF16),
            pltpu.VMEM((NZ, 16, 128), BF16),
            pltpu.VMEM((EX, T), F32),
            pltpu.VMEM((NE, T), F32),
            pltpu.VMEM((3, 8, T), F32),
            pltpu.VMEM((T, D), BF16),
            pltpu.VMEM((EX, T), F32),
            pltpu.VMEM((8, T), jnp.int32),
            dma((2, RE, 2)), dma((2, RE, 2)), dma((2, RE)), dma((2, RE)),
            one, dma((NN,)), one, dma((NN,)), one, dma((2,)), one, one, one, one,
            dma((NX - 1,)), dma((NX - 1,)), dma((NX,)), dma((NX,)),
            one, one, dma((NX - 1,)), dma((NX - 1,)), dma((NX,)), dma((NX,)),
            one, one, one, dma((NDP,)), one, one, dma((5,)),
        ],
        compiler_params=pltpu.CompilerParams(
            collective_id=0, has_side_effects=True, vmem_limit_bytes=58 * 2**20
        ),
        cost_estimate=pl.CostEstimate(flops=4 * 10**9, bytes_accessed=6 * 10**6, transcendentals=0),
    )(
        out_grad,
        router_logits.T,
        expert_ids.T,
        tokens_in,
        down_weight.reshape(FW // NDP, D),
        saved_hidden.reshape(NY, NZ * 8, FW),
    )
    return hid.reshape(1, 1, NE, 8, FW), lg.reshape(EX, T).T, rg.T


def solution(mesh, dims=(4, 4, 16)):
    in_specs = (
        P(("dp", "expert"), None),
        P(("dp", "expert"), None),
        P(("dp", "expert"), None),
        P(("dp", "expert"), None),
        P("dp", "expert", None, None, None),
        P("expert", "dp", None),
    )
    out_specs = (P("dp", "expert", None, None, None), P(("dp", "expert"), None), P("expert", "dp"))
    return jax.shard_map(
        functools.partial(local, dims), mesh=mesh, in_specs=in_specs, out_specs=out_specs, check_vma=False
    )
```

```python
import functools

import jax
import jax.numpy as jnp
from jax import lax
from jax.experimental import pallas as pl
from jax.experimental.pallas import tpu as pltpu
from jax.sharding import PartitionSpec as P

RSCALE = 2.827
ZLOSS = 0.25
NC = 2
MESH = pl.DeviceIdType.MESH
F32 = jnp.float32
BF16 = jnp.bfloat16


def drain(ref, sem):
    pltpu.make_async_copy(ref, ref, sem).wait()


def iota(shape, dim):
    return lax.broadcasted_iota(jnp.int32, shape, dim)


def kernel(
    dims,
    og_in, logits_in, ids_in, tok, w, saved,
    hid, lg, rg,
    ring, meta, nsend, nrecv, fsend, frecv, ftable, gnsend, gnrecv, gfsend, gfrecv, half,
    wfull, tokg, savedv, savedf, hidf, rsend, rrecv, esend, erecv, dsend, drecv, zsend, zrecv, zterm, posv, small, og, logits, ids,
    ring_s, ring_r, meta_s, meta_r, near_s, near_r, gn_s, gn_r, far_s, far_r, gf_s, gf_r, ret_s, ret_r,
    wx_s, wx_r, wc_s, wc_r, t1_s, t1_r, tx_s, tx_r, tc_s, tc_r, e_s, e_r, d_s, d_r, z_s, z_r, local_sem,
):
    NX, NY, NZ = dims
    NDP, NE = NX * NC, NY * NZ
    RE = NZ // 4
    NN, NF = 2 * RE + 1, 2 * RE - 1
    T, D = og_in.shape
    H = D // 2
    Q = D // NY
    FW = wfull.shape[0]
    FS = FW // NDP
    FC = min(FW, 256)
    EX = logits_in.shape[0]
    ED = EX // NDP
    R = D // NE
    dp, e = lax.axis_index("dp"), lax.axis_index("expert")
    x, core = dp // NC, dp % NC
    y, z = e // NZ, e % NZ
    nt = (((1,), (1,)), ((), ()))

    def remote(src, dst, s, r, dev):
        return pltpu.make_async_remote_copy(
            src_ref=src, dst_ref=dst, send_sem=s, recv_sem=r, device_id=dev, device_id_type=MESH
        )

    loads = [
        pltpu.make_async_copy(src, dst, local_sem.at[2 + i])
        for i, (src, dst) in enumerate(((logits_in, logits), (ids_in, ids), (og_in, og)))
    ]
    for copy in loads:
        copy.start()

    barrier = pltpu.get_barrier_semaphore()

    def greet(i, c):
        pl.semaphore_signal(barrier, inc=1, device_id=(dp, lax.rem(e + i, NE)), device_id_type=MESH)
        return c

    lax.fori_loop(1, NE, greet, 0)

    def greet2(i, c):
        other = lax.rem(dp + 1 + i // NY, NDP)
        pl.semaphore_signal(barrier, inc=1, device_id=(other, lax.rem(i, NY) * NZ + z), device_id_type=MESH)
        return c

    lax.fori_loop(0, (NDP - 1) * NY, greet2, 0)
    load = pltpu.make_async_copy(saved, savedv, local_sem.at[0])
    load.start()
    own_w = pltpu.make_async_copy(w, wfull.at[pl.ds(pl.multiple_of(dp * FS, FS), FS)], local_sem.at[1])
    own_w.start()

    loads[0].wait()
    loads[1].wait()
    lt = logits[...]
    top = jnp.max(lt, axis=0, keepdims=True)
    shifted = jnp.exp(lt - top)
    total = jnp.sum(shifted, axis=0, keepdims=True)
    lse = top + jnp.log(total)
    zterm[...] = (2.0 * ZLOSS) * lse * (shifted / total)
    names = iota((EX, T), 0)
    k_rows = [ids[k : k + 1, :] for k in range(8)]
    chosen = jnp.concatenate(
        [jnp.sum(jnp.where(names == row, lt, 0.0), axis=0, keepdims=True) for row in k_rows], axis=0
    )
    scores = 1.0 / (1.0 + jnp.exp(-chosen))
    ssum = jnp.sum(scores, axis=0, keepdims=True)
    gates = RSCALE * scores / ssum
    small[0] = scores
    small[1] = gates
    small[2] = jnp.broadcast_to(ssum, scores.shape)
    own_meta = meta.at[2 * RE]
    names_f = ids[...].astype(F32)
    own_meta[...] = jnp.concatenate([names_f, gates], axis=0).astype(BF16)
    for d in range(NDP):
        esend[d, :ED] = zterm[d * ED : (d + 1) * ED]
        esend[d, ED:] = names_f
    loads[2].wait()
    lane8 = iota((NY, 8, 128), 2) == iota((NY, 8, 128), 1)

    def slots(info):
        info = info.astype(F32)
        window = iota((NE, T), 0).astype(F32)
        mask = jnp.zeros((NE, T), F32)
        gate = jnp.zeros((NE, T), F32)
        for k in range(8):
            hit = window == info[k : k + 1, :]
            mask = jnp.where(hit, 1.0, mask)
            gate = jnp.where(hit, info[8 + k : 9 + k, :], gate)
        earlier = (iota((T, T), 0) < iota((T, T), 1)).astype(F32).astype(BF16)
        rank = jnp.dot(mask.astype(BF16), earlier, preferred_element_type=F32)
        return jnp.where(mask > 0.0, rank, 255.0), gate

    def tables(pos, gate, experts):
        n = experts.shape[0]
        pick = (iota((n, NE), 1) == experts).astype(F32).astype(BF16)
        spread = jnp.dot(pick, pos.astype(BF16), preferred_element_type=F32)
        hit = spread == (iota((n, T), 0) % 8).astype(F32)
        gates_at = jnp.dot(pick, gate.astype(BF16), preferred_element_type=F32)
        col = jnp.sum(jnp.where(hit, gates_at, 0.0), axis=1, keepdims=True).reshape(n // 8, 8, 1)
        at = iota((n // 8, 8, 128), 2) == iota((n // 8, 8, 128), 1)
        return hit.astype(F32).astype(BF16), jnp.sum(jnp.where(at, col, 0.0), axis=1, keepdims=True)

    def dispatch(ni, low, high, pos, gate):
        experts = iota((NY * 8, 1), 0) // 8 * NZ + z
        table, rows = tables(pos, gate, experts)
        gnsend[ni] = rows
        a = jnp.dot(table, low, preferred_element_type=F32).reshape(NY, 8, H)
        b = jnp.dot(table, high, preferred_element_type=F32).reshape(NY, 8, H)
        nsend[ni] = jnp.concatenate([a, b], axis=1).astype(BF16)
        for d in range(1, NY):
            yy = lax.rem(y + d, NY)
            remote(nsend.at[ni, yy], nrecv.at[ni, y], near_s, near_r.at[ni], (dp, yy * NZ + z)).start()
            remote(gnsend.at[ni, yy], gnrecv.at[ni, y], gn_s, gn_r.at[ni], (dp, yy * NZ + z)).start()
        pltpu.make_async_copy(nsend.at[ni, y], nrecv.at[ni, y], near_r.at[ni]).start()
        pltpu.make_async_copy(gnsend.at[ni, y], gnrecv.at[ni, y], gn_r.at[ni]).start()

    def hop(g, st, c):
        to = (dp, y * NZ + lax.rem(z + (1 if g == 0 else NZ - 1), NZ))
        src = og.at[:, pl.ds(c * H, H)] if st == 0 else ring.at[g, st - 1, c]
        remote(src, ring.at[g, st, c], ring_s.at[g, st, c], ring_r.at[g, st, c], to).start()
        if c == 0:
            info = own_meta if st == 0 else meta.at[g * RE + st - 1]
            remote(info, meta.at[g * RE + st], meta_s.at[g, st], meta_r.at[g, st], to).start()

    def arrived(g, st, c):
        if c == 0:
            drain(meta.at[g * RE + st], meta_r.at[g, st])
        drain(ring.at[g, st, c], ring_r.at[g, st, c])

    def relay(g, c):
        n = RE * NY
        if c == 0:
            d = iota((n * 8, 1), 0) // 8
            step = d // NY + 1
            experts = (y + d % NY) % NY * NZ + (z + (step if g == 0 else NZ - step)) % NZ
            pos, gate = slots(meta[g * RE + RE - 1])
            table, rows = tables(pos, gate, experts)
            ftable[g] = table
            gfsend[g] = rows
        p = jnp.dot(ftable[g], ring[g, RE - 1, c], preferred_element_type=F32).reshape(n, 8, H)
        fsend[c, g] = jnp.concatenate([p[:, :, : H // 2], p[:, :, H // 2 :]], axis=1).astype(BF16)

        def one(d, carry):
            j = d // NY + 1
            to = (dp, lax.rem(y + d % NY, NY) * NZ + lax.rem(z + (j if g == 0 else NZ - j), NZ))
            fi = j - 1 if g == 0 else jnp.where(j == RE, RE - 1, RE - 1 + j)
            remote(fsend.at[c, g, d], frecv.at[c, fi, y], far_s, far_r.at[c], to).start()
            if c == 0:
                remote(gfsend.at[g, d], gfrecv.at[fi, y], gf_s, gf_r, to).start()
            return carry

        last = (RE - 1) * NY
        split = last + NY // 2
        lax.fori_loop(*((last, split) if g == 0 else (split, RE * NY)), one, 0)
        lax.fori_loop(0, last, lambda i, carry: one(last - 1 - i, carry), 0)

    def w_rows(owner):
        return wfull.at[pl.ds(pl.multiple_of(owner * FS, FS), FS)]

    def tok_cols(yy):
        return tok.at[:, pl.ds(pl.multiple_of(yy * Q, 128), Q)]

    pair = (x * NC + 1 - core, e)
    own_w.wait()
    pl.semaphore_wait(barrier, NE - 1 + (NDP - 1) * NY)

    for c in range(2):
        for g in range(2):
            hop(g, 0, c)
    for d in range(1, NX):
        remote(w_rows(dp), w_rows(dp), wx_s.at[d - 1], wx_r.at[d - 1], (lax.rem(x + d, NX) * NC + core, e)).start()
    remote(w_rows(dp), w_rows(dp), wc_s.at[0], wc_r.at[0], pair).start()
    for d in range(1, NY):
        yy = lax.rem(y + d, NY)
        remote(tok_cols(yy), tokg.at[dp, y], t1_s, t1_r, (dp, yy * NZ + z)).start()
    pltpu.make_async_copy(tok_cols(y), tokg.at[dp, y], t1_r).start()

    mine = dp * NY + y

    def spread_early(i, c):
        to_dp, to_y = lax.rem(dp + i // NY, NDP), lax.rem(y + i, NY)
        remote(esend.at[to_dp], erecv.at[mine], e_s, e_r, (to_dp, to_y * NZ + z)).start()
        return c

    lax.fori_loop(1, NDP * NY, spread_early, 0)
    pltpu.make_async_copy(esend.at[dp], erecv.at[mine], e_r).start()

    pos, gate = slots(own_meta[...])
    posv[...] = pos
    dispatch(0, og[:, :H], og[:, H:], pos, gate)
    load.wait()
    savedf[...] = savedv[...].astype(F32).reshape(NY, NZ, 8, FW)

    for st in range(1, RE):
        for c in range(2):
            for g in range(2):
                arrived(g, st - 1, c)
                hop(g, st, c)
        for g in range(2):
            pos, gate = slots(meta[g * RE + st - 1])
            dispatch(2 * st - 1 + g, ring[g, st - 1, 0], ring[g, st - 1, 1], pos, gate)
        if st == max(RE - 2, 1):
            for d in range(1, NX):
                shard = lax.rem(x + NX - d, NX) * NC + core
                drain(w_rows(shard), wx_r.at[d - 1])
                remote(w_rows(shard), w_rows(shard), wc_s.at[d], wc_r.at[d], pair).start()
            drain(tokg.at[dp], t1_r)
            for d in range(1, NX):
                to = (lax.rem(x + d, NX) * NC + core, e)
                remote(tokg.at[dp], tokg.at[dp], tx_s.at[d - 1], tx_r.at[d - 1], to).start()
            remote(tokg.at[dp], tokg.at[dp], tc_s.at[0], tc_r.at[0], pair).start()

    def joined(block, n, width):
        v = block.astype(F32)
        low = v[:, :8].reshape(n * 8, width)
        high = v[:, 8:].reshape(n * 8, width)
        return jnp.concatenate([low, high], axis=1).astype(BF16)

    def finish(f, g, backs, columns, sources):
        for i, zs in enumerate(sources):
            part = g[i * NY * 8 : (i + 1) * NY * 8].reshape(NY, 8, FC)
            hidf[:, zs, :, f : f + FC] = columns[i] * part
            backs[i] = backs[i] + jnp.sum(savedf[:, zs, :, f : f + FC] * part, axis=2, keepdims=True)

    def column(rows):
        return jnp.sum(jnp.where(lane8, rows, 0.0), axis=2, keepdims=True)

    def give_back(i, zs, back):
        rsend[i] = jnp.sum(jnp.where(lane8, back, 0.0), axis=1, keepdims=True)
        for d in range(NY):
            yy = lax.rem(y + d, NY)
            if i == 0 and d == 0:
                pltpu.make_async_copy(rsend.at[i, yy], rrecv.at[e], ret_r).start()
            else:
                remote(rsend.at[i, yy], rrecv.at[e], ret_s, ret_r, (dp, yy * NZ + zs)).start()

    def near(group):
        sources = []
        for ni in group:
            drain(nrecv.at[ni], near_r.at[ni])
            drain(gnrecv.at[ni], gn_r.at[ni])
            st = (ni + 1) // 2
            sources.append(lax.rem(z + (NZ - st if ni % 2 == 1 else st), NZ))
        rows = jnp.concatenate([joined(nrecv[ni], NY, H) for ni in group], axis=0)
        columns = [column(gnrecv[ni]) for ni in group]
        backs = [jnp.zeros((NY, 8, 1), F32) for ni in group]
        for f in range(0, FW, FC):
            g = lax.dot_general(rows, wfull[f : f + FC], nt, preferred_element_type=F32)
            finish(f, g, backs, columns, sources)
        for ni, zs, back in zip(group, sources, backs):
            give_back(ni, zs, back)

    for c in range(2):
        for g in range(2):
            arrived(g, RE - 1, c)
            relay(g, c)
    for g in range(2):
        pos, gate = slots(meta[g * RE + RE - 1])
        dispatch(2 * RE - 1 + g, ring[g, RE - 1, 0], ring[g, RE - 1, 1], pos, gate)
    for d in range(NX):
        shard = lax.rem(x + NX - d, NX) * NC + 1 - core
        drain(w_rows(shard), wc_r.at[d])
    near([0, 1, 2])
    for first in range(3, NN, 4):
        near(list(range(first, min(first + 4, NN))))
    for d in range(1, NX):
        shard = lax.rem(x + NX - d, NX) * NC + core
        drain(tokg.at[shard], tx_r.at[d - 1])
        remote(tokg.at[shard], tokg.at[shard], tc_s.at[d], tc_r.at[d], pair).start()

    drain(frecv.at[0], far_r.at[0])
    rows = joined(frecv[0].reshape(NF * NY, 16, H // 2), NF * NY, H // 2)
    for f in range(0, FW, FC):
        half[:, f : f + FC] = lax.dot_general(rows, wfull[f : f + FC, :H], nt, preferred_element_type=F32)
    drain(gfrecv, gf_r)
    columns = [column(gfrecv[i]) for i in range(NF)]
    backs = [jnp.zeros((NY, 8, 1), F32) for i in range(NF)]
    sources = [lax.rem(z + (NZ - RE - 1 - i if i < RE else i + 1), NZ) for i in range(NF)]
    drain(frecv.at[1], far_r.at[1])
    rows = joined(frecv[1].reshape(NF * NY, 16, H // 2), NF * NY, H // 2)
    for f in range(0, FW, FC):
        g = lax.dot_general(rows, wfull[f : f + FC, H:], nt, preferred_element_type=F32)
        finish(f, g + half[:, f : f + FC], backs, columns, sources)
    for i in sorted(range(NF), key=lambda i: -(RE + 1 + i if i < RE else NZ - 1 - i)):
        give_back(NN + i, sources[i], backs[i])
    hid[...] = hidf[...].reshape(NY, NZ * 8, FW).astype(BF16)
    for d in range(NX):
        shard = lax.rem(x + NX - d, NX) * NC + 1 - core
        drain(tokg.at[shard], tc_r.at[d])

    drain(rrecv, ret_r)
    ret = rrecv[...].reshape(NE, 128)
    pos = posv[...]
    grad_e = jnp.zeros((NE, T), F32)
    for c in range(8):
        grad_e = jnp.where(pos == float(c), ret[:, c : c + 1], grad_e)
    scores, gates, ssum = small[0], small[1], small[2]
    k_rows = [ids[k : k + 1, :] for k in range(8)]
    window = iota((NE, T), 0)
    choice = jnp.concatenate(
        [jnp.sum(jnp.where(window == row, grad_e, 0.0), axis=0, keepdims=True) for row in k_rows], axis=0
    )
    mixed = jnp.sum(choice * gates, axis=0, keepdims=True) / RSCALE
    dchosen = RSCALE / ssum * (choice - mixed) * scores * (1.0 - scores)
    dsend[...] = dchosen

    def spread_d(i, c):
        i = lax.rem(i + NDP * NY // 2, NDP * NY)
        to_dp, to_y = lax.rem(dp + i // NY, NDP), lax.rem(y + i, NY)
        remote(dsend, drecv.at[mine], d_s, d_r.at[dp], (to_dp, to_y * NZ + z)).start()
        return c

    lax.fori_loop(0, NDP * NY // 2, spread_d, 0)
    lax.fori_loop(NDP * NY // 2 + 1, NDP * NY, spread_d, 0)
    pltpu.make_async_copy(dsend, drecv.at[mine], d_r.at[dp]).start()
    names = iota((EX, T), 0)
    lgt = zterm[...]
    for k, row in enumerate(k_rows):
        lgt = lgt + jnp.where(names == row, dchosen[k : k + 1, :], 0.0)
    lg[...] = lgt.reshape(NDP, ED, T)

    drain(erecv, e_r)
    own_names = (iota((ED, T), 0) + dp * ED).astype(F32)
    panel = jnp.zeros((2 * ED, Q), F32)
    for i in range(NDP):
        owner = lax.rem(dp + i, NDP)
        drain(drecv.at[pl.ds(owner * NY, NY)], d_r.at[owner])
        parts = []
        for yy in range(NY):
            at = owner * NY + yy
            early, late = erecv[at], drecv[at]
            v = early[:ED]
            for k in range(8):
                v = v + jnp.where(early[ED + k : ED + k + 1] == own_names, late[k : k + 1], 0.0)
            parts.append(v)
        v = jnp.concatenate(parts, axis=1)
        hi = v.astype(BF16).astype(F32)
        both = jnp.concatenate([v, v - hi], axis=0).astype(BF16)
        panel = panel + jnp.dot(both, tokg[owner].reshape(NY * T, Q), preferred_element_type=F32)
    panel = panel[:ED] + panel[ED:]
    blank = jnp.zeros((16, 64 - R), F32) if R < 64 else None
    for j in range(NZ):
        piece = panel[:, j * R : (j + 1) * R]
        sides = [piece[:16], jnp.concatenate([piece[16:], jnp.zeros((32 - ED, R), F32)], axis=0)]
        if R < 64:
            sides = [sides[0], blank, sides[1], blank]
        zsend[j] = jnp.concatenate(sides, axis=1).astype(BF16)

    def spread_z(i, c):
        step = (i + 1) // 2
        to = lax.rem(z + NZ // 2 + jnp.where(i % 2 == 1, NZ - step, step), NZ)
        remote(zsend.at[to], zrecv.at[z], z_s, z_r, (dp, y * NZ + to)).start()
        return c

    lax.fori_loop(0, NZ - 1, spread_z, 0)
    pltpu.make_async_copy(zsend.at[z], zrecv.at[z], z_r).start()
    drain(zrecv, z_r)
    out = jnp.sum(zrecv[...].astype(F32), axis=0)
    rg[:16] = out[:, :R]
    rg[16:] = out[: ED - 16, 64 : 64 + R]

    for g in range(2):
        for st in range(RE):
            drain(meta.at[0], meta_s.at[g, st])
            for c in range(2):
                drain(ring.at[0, 0, 0], ring_s.at[g, st, c])
    drain(nsend.at[:, pl.ds(0, NY - 1)], near_s)
    drain(gnsend.at[:, pl.ds(0, NY - 1)], gn_s)
    drain(frecv, far_s)
    drain(gfrecv, gf_s)
    drain(rsend.at[pl.ds(1, NZ - 1)], ret_s)
    drain(rsend.at[0, pl.ds(0, NY - 1)], ret_s)
    for d in range(NX - 1):
        drain(w_rows(dp), wx_s.at[d])
        drain(tokg.at[dp], tx_s.at[d])
    for d in range(NX):
        drain(w_rows(dp), wc_s.at[d])
        drain(tokg.at[dp], tc_s.at[d])
    drain(tokg.at[dp, pl.ds(0, NY - 1)], t1_s)
    drain(erecv.at[pl.ds(0, NDP * NY - 1)], e_s)
    drain(drecv.at[pl.ds(0, NDP * NY - 1)], d_s)
    drain(zsend.at[pl.ds(0, NZ - 1)], z_s)


def local(dims, tokens_in, out_grad, router_logits, expert_ids, saved_hidden, down_weight):
    NX, NY, NZ = dims
    NDP, NE = NX * NC, NY * NZ
    RE = NZ // 4
    NN, NF = 2 * RE + 1, 2 * RE - 1
    T, D = out_grad.shape
    H = D // 2
    FW = saved_hidden.shape[4]
    EX = router_logits.shape[1]
    ED, Q, R = EX // NDP, D // NY, D // NE
    vmem = pl.BlockSpec(memory_space=pltpu.VMEM)
    hbm = pl.BlockSpec(memory_space=pl.ANY)
    dma = pltpu.SemaphoreType.DMA
    one = dma(())
    hid, lg, rg = pl.pallas_call(
        functools.partial(kernel, dims),
        out_shape=(
            pltpu.VMEM((NY, NZ * 8, FW), BF16),
            pltpu.VMEM((NDP, ED, T), F32),
            pltpu.VMEM((ED, R), F32),
        ),
        in_specs=[hbm] * 6,
        out_specs=(vmem, vmem, vmem),
        scratch_shapes=[
            pltpu.VMEM((2, RE, 2, T, H), BF16),
            pltpu.VMEM((2 * RE + 1, 16, T), BF16),
            pltpu.VMEM((NN, NY, 16, H), BF16),
            pltpu.VMEM((NN, NY, 16, H), BF16),
            pltpu.VMEM((2, 2, RE * NY, 16, H // 2), BF16),
            pltpu.VMEM((2, NF, NY, 16, H // 2), BF16),
            pltpu.VMEM((2, RE * NY * 8, T), BF16),
            pltpu.VMEM((NN, NY, 1, 128), F32),
            pltpu.VMEM((NN, NY, 1, 128), F32),
            pltpu.VMEM((2, RE * NY, 1, 128), F32),
            pltpu.VMEM((NF, NY, 1, 128), F32),
            pltpu.VMEM((NF * NY * 8, FW), F32),
            pltpu.VMEM((FW, D), BF16),
            pltpu.VMEM((NDP, NY, T, Q), BF16),
            pltpu.VMEM((NY, NZ * 8, FW), BF16),
            pltpu.VMEM((NY, NZ, 8, FW), F32),
            pltpu.VMEM((NY, NZ, 8, FW), F32),
            pltpu.VMEM((NZ, NY, 1, 128), F32),
            pltpu.VMEM((NE, 1, 128), F32),
            pltpu.VMEM((NDP, ED + 8, T), F32),
            pltpu.VMEM((NDP * NY, ED + 8, T), F32),
            pltpu.VMEM((8, T), F32),
            pltpu.VMEM((NDP * NY, 8, T), F32),
            pltpu.VMEM((NZ, 16, 128), BF16),
            pltpu.VMEM((NZ, 16, 128), BF16),
            pltpu.VMEM((EX, T), F32),
            pltpu.VMEM((NE, T), F32),
            pltpu.VMEM((3, 8, T), F32),
            pltpu.VMEM((T, D), BF16),
            pltpu.VMEM((EX, T), F32),
            pltpu.VMEM((8, T), jnp.int32),
            dma((2, RE, 2)), dma((2, RE, 2)), dma((2, RE)), dma((2, RE)),
            one, dma((NN,)), one, dma((NN,)), one, dma((2,)), one, one, one, one,
            dma((NX - 1,)), dma((NX - 1,)), dma((NX,)), dma((NX,)),
            one, one, dma((NX - 1,)), dma((NX - 1,)), dma((NX,)), dma((NX,)),
            one, one, one, dma((NDP,)), one, one, dma((5,)),
        ],
        compiler_params=pltpu.CompilerParams(
            collective_id=0, has_side_effects=True, vmem_limit_bytes=58 * 2**20
        ),
        cost_estimate=pl.CostEstimate(flops=4 * 10**9, bytes_accessed=6 * 10**6, transcendentals=0),
    )(
        out_grad,
        router_logits.T,
        expert_ids.T,
        tokens_in,
        down_weight.reshape(FW // NDP, D),
        saved_hidden.reshape(NY, NZ * 8, FW),
    )
    return hid.reshape(1, 1, NE, 8, FW), lg.reshape(EX, T).T, rg.T


def solution(mesh, dims=(4, 4, 16)):
    in_specs = (
        P(("dp", "expert"), None),
        P(("dp", "expert"), None),
        P(("dp", "expert"), None),
        P(("dp", "expert"), None),
        P("dp", "expert", None, None, None),
        P("expert", "dp", None),
    )
    out_specs = (P("dp", "expert", None, None, None), P(("dp", "expert"), None), P("expert", "dp"))
    return jax.shard_map(
        functools.partial(local, dims), mesh=mesh, in_specs=in_specs, out_specs=out_specs, check_vma=False
    )
```
